512 devices in a mesh: cuts: 32 (over x, z_hi, core), chip: 16 (over y, z_lo).
Axes of the slice: x: 4, y: 8, z: 8 (z_hi: 4, z_lo: 2; z = z_hi * 2 + z_lo), core: 2. Of those that a mesh axis runs over, the one named last changes fastest.
Arguments:
- hidden: bfloat16 [65536, 5120], P(('cuts', 'chip')), may hold values from -8 to 8
- out_grad: bfloat16 [65536, 5120], P(('cuts', 'chip')), may hold values from -24 to 24
- weights: bfloat16 [4, 5120, 128], P(None, 'chip'), may hold values from -0.078125 to 0.078125
Outputs:
- input_grad: bfloat16 [65536, 5120], P(('cuts', 'chip'))
- weight_grads: float32 [4, 5120, 128], P(None, ('cuts', 'chip'))
The draws below stay inside these ranges and needn't reach their ends.
All inputs are finite; a program needn't handle non-finite values.
Results may differ from the reference program's by a relative error of at most 0.039.
Values may be sent and summed in bfloat16 or wider, within the bound.
A program may use at most 64 MiB of HBM per device.

```python
import math
import jax
import jax.numpy as jnp
from jax import lax

D = 5120
HD = 128
SEQ = 128
TOKENS = 65536


def draw_hidden(key, part):
    key = jax.random.fold_in(key, 11)
    first, second = jax.random.split(key)
    entries = jnp.clip(jax.random.normal(first, (TOKENS, D), jnp.float32), -4.0, 4.0)
    scales = jnp.exp(jax.random.uniform(second, (TOKENS, 1), jnp.float32, math.log(0.5), math.log(2.0)))
    return (entries * scales).astype(jnp.bfloat16)


def raised(result, key, source, target, shards_of, factor):
    def block_of(dim):
        return (jnp.arange(result.shape[dim]) // (result.shape[dim] // shards_of)).reshape((-1,) + (1,) * (result.ndim - 1 - dim))

    near = jax.random.permutation(key, shards_of)[block_of(target)]
    other_side = (block_of(target) + shards_of // 2) % shards_of
    return jnp.where((block_of(source) == near) | (block_of(source) == other_side), factor * result, result)


def steps_of(own_key, extent, shards, smallest, largest):
    def one(dim, shards_of):
        steps = jax.random.uniform(jax.random.fold_in(jax.random.fold_in(own_key, 6), dim), (shards_of,), jnp.float32, smallest / len(shards), largest / len(shards))
        return jnp.repeat(jnp.exp(steps), extent[dim] // shards_of).reshape((-1,) + (1,) * (len(extent) - dim - 1))

    gain = one(*shards[0])
    for cut in shards[1:]:
        gain = gain * one(*cut)
    return gain


def bell_draw(rng, shape, deviation, bound, shards=(), kind=jnp.bfloat16):
    array = jax.random.normal(rng, shape, jnp.float32) * deviation
    if len(shards) > 0:
        array = steps_of(rng, shape, shards, -0.22, 0.18) * array
    return jnp.clip(array, min=-bound, max=bound).astype(kind)


def bell_draw_with(key, dims, spread, limit, cuts, heavy, kind=jnp.bfloat16):
    drawn = spread * jax.random.normal(key, dims, jnp.float32)
    if cuts:
        drawn = drawn * steps_of(key, dims, cuts, -0.22, 0.18)
    return jnp.clip(raised(drawn, jax.random.fold_in(key, 3), *heavy), -limit, limit).astype(kind)


def setup_inputs(seed: int = 0) -> dict:
    arg_keys = jax.random.split(jax.random.key(seed), 4)
    hidden = draw_hidden(jax.random.fold_in(arg_keys[3], 71), 0)
    out_grad = bell_draw_with(arg_keys[1], (TOKENS, D), 1.0, 24.0, ((0, 512),), (0, 1, 512, 6.0))
    weights = bell_draw(arg_keys[2], (4, D, HD), D ** -0.5, 0.078125, ((1, 16),))
    return {"hidden": hidden, "out_grad": out_grad, "weights": weights}


def rope_tables(length, width):
    half = width // 2
    position = jnp.arange(length, dtype=jnp.float32)[:, None]
    rates = 10000.0 ** (-(jnp.arange(half, dtype=jnp.float32) * 2.0) / width)
    angle = position * rates[None, :]
    return (jnp.cos(angle), jnp.sin(angle))

def rotate(values, cosine, sine, flip):
    half = values.shape[1] // 2
    first = values[:, :half]
    second = values[:, half:]
    sine = sine * flip
    return jnp.concatenate([first * cosine - second * sine, second * cosine + first * sine], axis=1)

def one_sequence(hidden, out_grad, weights):
    w_query, w_key, w_value, w_out = (weights[0], weights[1], weights[2], weights[3])
    length, width = (hidden.shape[0], w_query.shape[1])
    cosine, sine = rope_tables(length, width)
    scale = 1.0 / jnp.sqrt(jnp.float32(width))
    query = rotate(jnp.dot(hidden, w_query, preferred_element_type=jnp.float32), cosine, sine, 1.0).astype(jnp.bfloat16)
    keys = rotate(jnp.dot(hidden, w_key, preferred_element_type=jnp.float32), cosine, sine, 1.0).astype(jnp.bfloat16)
    values = jnp.dot(hidden, w_value, preferred_element_type=jnp.float32).astype(jnp.bfloat16)
    scores = jnp.dot(query, keys.T, preferred_element_type=jnp.float32) * scale
    rows = jnp.arange(length)[:, None]
    cols = jnp.arange(length)[None, :]
    scores = jnp.where(cols <= rows, scores, -jnp.inf)
    top = lax.optimization_barrier(jnp.max(scores, axis=1, keepdims=True))
    expo = jnp.exp(scores - top)
    prob = expo / lax.optimization_barrier(jnp.sum(expo, axis=1, keepdims=True))
    prob_b = prob.astype(jnp.bfloat16)
    attn = jnp.dot(prob_b, values, preferred_element_type=jnp.float32).astype(jnp.bfloat16)
    d_attn = jnp.dot(out_grad, w_out, preferred_element_type=jnp.float32).astype(jnp.bfloat16)
    d_prob = jnp.dot(d_attn, values.T, preferred_element_type=jnp.float32)
    d_score = (prob * (d_prob - lax.optimization_barrier(jnp.sum(prob * d_prob, axis=1, keepdims=True))) * scale).astype(jnp.bfloat16)
    d_query = rotate(jnp.dot(d_score, keys, preferred_element_type=jnp.float32), cosine, sine, -1.0).astype(jnp.bfloat16)
    d_key = rotate(jnp.dot(d_score.T, query, preferred_element_type=jnp.float32), cosine, sine, -1.0).astype(jnp.bfloat16)
    d_value = jnp.dot(prob_b.T, d_attn, preferred_element_type=jnp.float32).astype(jnp.bfloat16)
    input_grad = (jnp.dot(d_query, w_query.T, preferred_element_type=jnp.float32) + jnp.dot(d_key, w_key.T, preferred_element_type=jnp.float32) + jnp.dot(d_value, w_value.T, preferred_element_type=jnp.float32)).astype(jnp.bfloat16)
    partial_value = jnp.stack([jnp.dot(hidden.T, d_query, preferred_element_type=jnp.float32), jnp.dot(hidden.T, d_key, preferred_element_type=jnp.float32), jnp.dot(hidden.T, d_value, preferred_element_type=jnp.float32), jnp.dot(out_grad.T, attn, preferred_element_type=jnp.float32)]).astype(jnp.bfloat16)
    return (input_grad, partial_value)

def reference(hidden, out_grad, weights):
    count = TOKENS // SEQ
    hidden_seq = hidden.reshape(count, SEQ, D)
    grad_seq = out_grad.reshape(count, SEQ, D)

    def step(total, pair):
        input_grad, partial_value = one_sequence(pair[0], pair[1], weights)
        return (total + partial_value.astype(jnp.float32), input_grad)
    start = jnp.zeros((4, D, HD), jnp.float32)
    total, input_grads = lax.scan(step, start, (hidden_seq, grad_seq))
    return (input_grads.reshape(TOKENS, D), total / jnp.float32(count))
```

```python
import jax
import jax.numpy as jnp
import numpy as np
from jax import lax
from jax.experimental import pallas as pl
from jax.experimental.pallas import tpu as pltpu
from jax.sharding import PartitionSpec as P

MESH = pl.DeviceIdType.MESH
F32 = jnp.float32
BF16 = jnp.bfloat16

HD = 128
SEQ = 128
HALF = 2560
ITEM = 640
CHUNK = 1280
BLOCK = 160


def rope_tables():
    half = HD // 2
    rates = 10000.0 ** (-(np.arange(half) * 2.0) / HD)
    angle = np.arange(SEQ)[:, None] * rates[None, :]
    cosine, sine = np.cos(angle), np.sin(angle)
    return (
        np.concatenate([cosine, cosine], axis=1).astype(np.float32),
        np.concatenate([-sine, sine], axis=1).astype(np.float32),
    )


def dot(a, b):
    return jnp.dot(a, b, preferred_element_type=F32)


def dot_nt(a, b):
    return lax.dot_general(a, b, (((1,), (1,)), ((), ())), preferred_element_type=F32)


def kernel(
    hid, og, wts, cosr, sinr, ig_out, wg_out,
    Hb, Ob, W, HT, OT, acc, accr, DD, PP, Ropp, Rn, Ro, Sb, Rz, T, U, Ru, IG,
    loc_sem, sib_s, sib_r, g1_s, g1_r, g2_s, g2_r,
    opp_s, opp_r, nb_s, nb_r, own_s, own_r, z_s, z_r, y_s, y_r,
):
    ci = lax.axis_index("cuts")
    ch = lax.axis_index("chip")
    x = ci // 8
    zh = (ci // 2) % 4
    c = ci % 2
    y = ch // 2
    zl = ch % 2
    z = zh * 2 + zl
    o = 1 - c

    def dev(x_, y_, z_, c_):
        return (x_ * 8 + (z_ // 2) * 2 + c_, y_ * 2 + z_ % 2)

    def rcopy(src, dst, ss, rs, to):
        return pltpu.make_async_remote_copy(
            src_ref=src, dst_ref=dst, send_sem=ss, recv_sem=rs, device_id=to, device_id_type=MESH
        )

    sib = dev(x, y, z, o)
    active = y // 4 == c
    base = pl.multiple_of((y % 4) * ITEM + zl * 320, 32)
    base_o = pl.multiple_of((y % 4) * ITEM + (1 - zl) * 320, 32)
    mine = pl.ds(pl.multiple_of(c * SEQ, SEQ), SEQ)
    theirs = pl.ds(pl.multiple_of(o * SEQ, SEQ), SEQ)
    col_c = pl.ds(pl.multiple_of(c * HALF, HALF), HALF)
    col_o = pl.ds(pl.multiple_of(o * HALF, HALF), HALF)

    lh = pltpu.make_async_copy(hid.at[:, col_c], Hb.at[mine, :], loc_sem.at[0])
    lo = pltpu.make_async_copy(og.at[:, col_c], Ob.at[mine, :], loc_sem.at[1])
    lw = pltpu.make_async_copy(wts, W.at[:, pl.ds(base, 320), :], loc_sem.at[2])

    @pl.when(active)
    def _():
        lw.start()

    lh.start()
    lo.start()

    bar = pltpu.get_barrier_semaphore()

    def greet(to):
        pl.semaphore_signal(bar, inc=1, device_id=to, device_id_type=MESH)

    greet(sib)
    for dx in (1, 3):
        for cc in (0, 1):
            greet(dev((x + dx) % 4, y, z, cc))
    for dz in range(1, 8):
        greet(dev(x, y, (z + dz) % 8, c))
    for dy in range(1, 8):
        for l in (0, 1):
            greet(dev(x, (y + dy) % 8, zh * 2 + l, c))
    acc[...] = jnp.zeros_like(acc)
    T[...] = jnp.zeros_like(T)
    pl.semaphore_wait(bar, 1 + 4 + 7 + 14)

    zp, zm = (z + 1) % 8, (z + 7) % 8
    g1 = [
        rcopy(
            wts.at[:, pl.ds(160 * i, 160), :],
            W.at[:, pl.ds(base + 160 * i, 160), :],
            g1_s.at[i], g1_r.at[i], dev(x, y, (zp, zm)[i], c),
        )
        for i in range(2)
    ]

    @pl.when(active)
    def _():
        g1[0].start()
        g1[1].start()

    sh = rcopy(hid.at[:, col_o], Hb.at[mine, :], sib_s.at[0], sib_r.at[0], sib)
    so = rcopy(og.at[:, col_o], Ob.at[mine, :], sib_s.at[1], sib_r.at[1], sib)
    sh.start()
    so.start()

    yp, ym = (y + 1) % 8, (y + 7) % 8

    def item_ref(s, sub):
        return W.at[pl.ds(2 * sub, 2), pl.ds(pl.multiple_of((s % 4) * ITEM, 128), ITEM), :]

    def forward(s, t, d, sub):
        r = item_ref(s, sub)
        return rcopy(
            r, r, g2_s.at[t, d, sub], g2_r.at[s % 4, sub], dev(x, (yp, ym)[d], z, c)
        )

    def arrived(s, sub):
        r = item_ref(s, sub)
        rcopy(r, r, g2_s.at[0, 0, sub], g2_r.at[s % 4, sub], dev(x, yp, z, c)).wait_recv()

    def project(s):
        at = pl.ds(pl.multiple_of((s % 4) * ITEM, 128), ITEM)
        wq = jnp.concatenate([W[0, at, :], W[1, at, :], W[2, at, :]], axis=1)
        acc[:, 0:384] += dot(Hb[:, at], wq)
        acc[:, 384:512] += dot(Ob[:, at], W[3, at, :])

    def transpose(src, dst, q):
        turned = src[:, q * ITEM : (q + 1) * ITEM].T
        for i in range(4):
            zr, cr = (q % 2) * 2 + i // 2, i % 2
            at = (q // 2) * CHUNK + (cr * 4 + zr) * BLOCK
            dst[at : at + BLOCK, :] = turned[i * BLOCK : (i + 1) * BLOCK, :]

    @pl.when(active)
    def _():
        lw.wait()
        for i in range(2):
            rcopy(
                wts.at[:, pl.ds(160 * i, 160), :],
                W.at[:, pl.ds(base_o + 160 * i, 160), :],
                g1_s.at[i], g1_r.at[i], dev(x, y, (zp, zm)[i], c),
            ).wait_recv()
        for sub, d in ((0, 0), (1, 1), (1, 0), (0, 1)):
            forward(y, 0, d, sub).start()

    lh.wait()
    sh.wait_recv()
    for q in range(4):
        transpose(Hb, HT, q)
    lo.wait()
    so.wait_recv()

    @pl.when(active)
    def _():
        project(y)

    for t in range(1, 5):
        sources = ((y + 8 - t) % 8, (y + t) % 8)
        if t < 4:
            for sub in (0, 1):
                for d in (0, 1):
                    s = sources[d]
                    sb = sub if d == 0 else 1 - sub

                    @pl.when(s // 4 == c)
                    def _():
                        arrived(s, sb)
                        if t < 3 or sb == d:
                            forward(s, t, d, sb).start()

            if t == 1:
                for q in range(4):
                    transpose(Ob, OT, q)
            for d in (0, 1):
                s = sources[d]

                @pl.when(s // 4 == c)
                def _():
                    project(s)

        else:
            s = sources[0]

            @pl.when(s // 4 == c)
            def _():
                arrived(s, 0)
                arrived(s, 1)
                project(s)

    sa = rcopy(acc.at[theirs, :], accr, sib_s.at[2], sib_r.at[2], sib)
    sa.start()
    cosine, sine = cosr[...], sinr[...]

    def rope(v, sgn):
        return v * cosine + pltpu.roll(v, 64, 1) * (sine * sgn)

    scale = 1.0 / np.sqrt(np.float32(HD))
    rows = lax.broadcasted_iota(jnp.int32, (SEQ, SEQ), 0)
    cols = lax.broadcasted_iota(jnp.int32, (SEQ, SEQ), 1)
    sa.wait_recv()
    summed = acc[mine, :] + accr[...]
    query = rope(summed[:, 0:128], 1.0).astype(BF16)
    keys = rope(summed[:, 128:256], 1.0).astype(BF16)
    values = summed[:, 256:384].astype(BF16)
    d_attn = summed[:, 384:512].astype(BF16)
    scores = dot_nt(query, keys) * scale
    d_prob = dot_nt(d_attn, values)
    scores = jnp.where(cols <= rows, scores, -jnp.inf)
    expo = jnp.exp(scores - jnp.max(scores, axis=1, keepdims=True))
    prob = expo / jnp.sum(expo, axis=1, keepdims=True)
    prob_b = prob.astype(BF16)
    attn = dot(prob_b, values)
    d_score = prob * (d_prob - jnp.sum(prob * d_prob, axis=1, keepdims=True)) * scale
    d_query = rope(dot(d_score.astype(BF16), keys), -1.0)
    d_key = rope(dot(d_score.T.astype(BF16), query), -1.0)
    d_value = dot(prob.T.astype(BF16), d_attn)
    DD[mine, :] = jnp.concatenate([d_query, d_key, d_value, attn], axis=1).astype(BF16)
    sd = rcopy(DD.at[mine, :], DD.at[mine, :], sib_s.at[3], sib_r.at[3], sib)
    sd.start()
    rcopy(DD.at[theirs, :], DD.at[theirs, :], sib_s.at[3], sib_r.at[3], sib).wait_recv()

    dd = (2 * c + 4 - x) % 4
    is_opp = (dd == 1) | (dd == 2)
    plus = dd < 2
    kn = jnp.where((dd == 0) | (dd == 2), 1, 0)
    ks = 1 - kn
    xn = jnp.where(plus, (x + 1) % 4, (x + 3) % 4)
    xp, xm = (x + 1) % 4, (x + 3) % 4
    slot = jnp.where(plus, 0, 1)
    lane_f = pl.multiple_of(jnp.where(plus, 0, 256), 256)
    lane_d = pl.multiple_of(jnp.where(plus, 256, 0), 256)

    def piece(k, rb):
        at = pl.ds(pl.multiple_of(k * CHUNK + rb * BLOCK, 32), BLOCK)
        left = dot(HT[at, :], DD[:, 0:384])
        right = dot(OT[at, :], DD[:, 384:512])
        return at, left.astype(BF16), right.astype(BF16)

    def opp_copy(rb, h):
        return rcopy(
            PP.at[pl.ds(pl.multiple_of(ks * CHUNK + rb * BLOCK, 32), BLOCK), pl.ds(256 * h, 256)],
            Ropp.at[pl.ds(pl.multiple_of(rb * BLOCK, 32), BLOCK), :],
            opp_s.at[rb, h], opp_r.at[rb], dev((xp, xm)[h], y, z, c),
        )

    def nb_copy(rb, h, lane):
        cr, zr = rb // 4, rb % 4
        return rcopy(
            PP.at[pl.ds(pl.multiple_of(kn * CHUNK + rb * BLOCK, 32), BLOCK), pl.ds(lane, 256)],
            Rn.at[slot, pl.ds(pl.multiple_of(zr * BLOCK, 32), BLOCK), pl.ds(lane, 256)],
            nb_s.at[rb, h], nb_r.at[slot, zr, lane // 256], dev(xn, y, z, cr),
        )

    def own_copy(zr):
        return rcopy(
            PP.at[pl.ds(pl.multiple_of(ks * CHUNK + (o * 4 + zr) * BLOCK, 32), BLOCK), :],
            Ro.at[pl.ds(pl.multiple_of(zr * BLOCK, 32), BLOCK), :],
            own_s.at[zr], own_r.at[zr], sib,
        )

    @pl.when(is_opp)
    def _():
        @pl.loop(0, 8)
        def _(rb):
            at, left, right = piece(ks, rb)
            PP[at, 0:384] = left
            PP[at, 384:512] = right
            opp_copy(rb, 0).start()
            opp_copy(rb, 1).start()

    @pl.loop(0, 8)
    def _(rb):
        at, left, right = piece(kn, rb)
        PP[at, 0:384] = left
        PP[at, 384:512] = right
        nb_copy(rb, 1, lane_d).start()

    @pl.when(jnp.logical_not(is_opp))
    def _():
        @pl.loop(0, 4)
        def _(zr):
            at, left, right = piece(ks, o * 4 + zr)
            PP[at, 0:384] = left
            PP[at, 384:512] = right
            own_copy(zr).start()

        @pl.loop(0, 4)
        def _(zr):
            at, left, right = piece(ks, c * 4 + zr)
            to = pl.ds(pl.multiple_of(zr * BLOCK, 32), BLOCK)
            Ro[to, 0:384] = left
            Ro[to, 384:512] = right

    @pl.loop(0, 8)
    def _(rb):
        opp_copy(rb, 0).wait_recv()
        at = pl.ds(pl.multiple_of(kn * CHUNK + rb * BLOCK, 32), BLOCK)
        lanes = pl.ds(lane_f, 256)
        got = Ropp[pl.ds(pl.multiple_of(rb * BLOCK, 32), BLOCK), :]
        PP[at, lanes] = (PP[at, lanes].astype(F32) + got.astype(F32)).astype(BF16)
        nb_copy(rb, 0, lane_f).start()

    @pl.loop(0, 4)
    def _(q):
        at = pl.ds(pl.multiple_of(q * ITEM, 128), ITEM)
        wq = jnp.concatenate([W[0, at, :], W[1, at, :], W[2, at, :]], axis=1)
        IG[:, at] = dot_nt(DD[:, 0:384], wq).astype(BF16)

    li = pltpu.make_async_copy(IG.at[mine, :], ig_out.at[:, col_c], loc_sem.at[3])
    li.start()
    si = rcopy(IG.at[theirs, :], ig_out.at[:, col_c], sib_s.at[4], sib_r.at[4], sib)
    si.start()

    def z_copy(b):
        return rcopy(
            Sb.at[pl.ds(pl.multiple_of(b * 80, 16), 80), :],
            Rz.at[z], z_s.at[b], z_r.at[z], dev(x, y, b, c),
        )

    @pl.loop(0, 4)
    def _(zr):
        at = pl.ds(pl.multiple_of(zr * BLOCK, 32), BLOCK)

        @pl.when(is_opp)
        def _():
            own_copy(zr).wait_recv()

        for src in (0, 1):
            for h in (0, 1):
                rcopy(
                    Rn.at[src, at, pl.ds(256 * h, 256)],
                    Rn.at[src, at, pl.ds(256 * h, 256)],
                    nb_s.at[0, 0], nb_r.at[src, zr, h], sib,
                ).wait_recv()
        total = Ro[at, :].astype(F32) + Rn[0, at, :].astype(F32) + Rn[1, at, :].astype(F32)
        Sb[at, :] = total.astype(BF16)
        for s in (0, 1):
            b = zr * 2 + s

            @pl.when(b != z)
            def _():
                z_copy(b).start()

    Rz[z] = Sb[pl.ds(pl.multiple_of(z * 80, 16), 80), :]

    @pl.loop(0, 8)
    def _(k):
        @pl.when(k != z)
        def _():
            rcopy(
                Sb.at[pl.ds(pl.multiple_of(k * 80, 16), 80), :],
                Rz.at[k], z_s.at[k], z_r.at[k], dev(x, y, k, c),
            ).wait_recv()

        T[0:80, :] = T[0:80, :] + Rz[k].astype(F32)

    def y_copy(k):
        yr, lr = zl * 4 + k // 2, k % 2
        return rcopy(U.at[k], Ru.at[y], y_s.at[k], y_r.at[y], dev(x, yr, zh * 2 + lr, c))

    self_k = (y % 4) * 2 + zl
    feeds_self = zl == y // 4
    for k in range(8):
        unit = T[10 * k : 10 * k + 16, :].astype(BF16)
        U[k] = unit
        to_self = feeds_self & (self_k == k)

        @pl.when(to_self)
        def _():
            Ru[y] = unit

        @pl.when(jnp.logical_not(to_self))
        def _():
            y_copy(k).start()

    total = None
    for k in range(8):
        @pl.when(jnp.logical_not(feeds_self & (y == k)))
        def _():
            rcopy(
                U.at[k], Ru.at[k], y_s.at[k], y_r.at[k], dev(x, k, zh * 2 + 1 - zl, c)
            ).wait_recv()

        part = Ru[k].astype(F32)
        total = part if total is None else total + part
    total = total * (1.0 / 512.0)
    for j in range(4):
        wg_out[j] = total[0:10, 128 * j : 128 * j + 128]

    li.wait()
    si.wait()
    sh.wait_send()
    so.wait_send()
    sa.wait_send()
    sd.wait_send()

    @pl.when(active)
    def _():
        g1[0].wait_send()
        g1[1].wait_send()
        for sub, d in ((0, 0), (1, 1), (1, 0), (0, 1)):
            forward(y, 0, d, sub).wait_send()

    for t in range(1, 4):
        sources = ((y + 8 - t) % 8, (y + t) % 8)
        for d in (0, 1):
            s = sources[d]

            @pl.when(s // 4 == c)
            def _():
                for sub in (0, 1):
                    if t < 3 or sub == d:
                        forward(s, t, d, sub).wait_send()

    @pl.loop(0, 8)
    def _(rb):
        nb_copy(rb, 0, lane_f).wait_send()
        nb_copy(rb, 1, lane_d).wait_send()

        @pl.when(is_opp)
        def _():
            opp_copy(rb, 0).wait_send()
            opp_copy(rb, 1).wait_send()

        @pl.when(rb != z)
        def _():
            z_copy(rb).wait_send()

        @pl.when(jnp.logical_not(feeds_self & (self_k == rb)))
        def _():
            y_copy(rb).wait_send()

    @pl.when(jnp.logical_not(is_opp))
    def _():
        @pl.loop(0, 4)
        def _(zr):
            own_copy(zr).wait_send()


def local(hidden, out_grad, weights):
    cosine, sine = rope_tables()
    vmem = pl.BlockSpec(memory_space=pltpu.VMEM)
    anyspace = pl.BlockSpec(memory_space=pl.ANY)
    dma = pltpu.SemaphoreType.DMA
    return pl.pallas_call(
        kernel,
        out_shape=(
            jax.ShapeDtypeStruct(hidden.shape, BF16),
            jax.ShapeDtypeStruct((4, 10, HD), F32),
        ),
        in_specs=[anyspace, anyspace, anyspace, vmem, vmem],
        out_specs=(anyspace, vmem),
        scratch_shapes=[
            pltpu.VMEM((256, HALF), BF16),
            pltpu.VMEM((256, HALF), BF16),
            pltpu.VMEM((4, HALF, HD), BF16),
            pltpu.VMEM((HALF, 256), BF16),
            pltpu.VMEM((HALF, 256), BF16),
            pltpu.VMEM((256, 512), F32),
            pltpu.VMEM((SEQ, 512), F32),
            pltpu.VMEM((256, 512), BF16),
            pltpu.VMEM((HALF, 512), BF16),
            pltpu.VMEM((CHUNK, 256), BF16),
            pltpu.VMEM((2, 640, 512), BF16),
            pltpu.VMEM((640, 512), BF16),
            pltpu.VMEM((640, 512), BF16),
            pltpu.VMEM((8, 80, 512), BF16),
            pltpu.VMEM((96, 512), F32),
            pltpu.VMEM((8, 16, 512), BF16),
            pltpu.VMEM((8, 16, 512), BF16),
            pltpu.VMEM((256, HALF), BF16),
            dma((4,)),
            dma((5,)), dma((5,)),
            dma((2,)), dma((2,)),
            dma((4, 2, 2)), dma((4, 2)),
            dma((8, 2)), dma((8,)),
            dma((8, 2)), dma((2, 4, 2)),
            dma((4,)), dma((4,)),
            dma((8,)), dma((8,)),
            dma((8,)), dma((8,)),
        ],
        compiler_params=pltpu.CompilerParams(
            collective_id=0, has_side_effects=True, vmem_limit_bytes=48 * 1024 * 1024
        ),
    )(hidden, out_grad, weights, cosine, sine)


def solution(mesh):
    placed = (P(("cuts", "chip"), None), P(("cuts", "chip"), None), P(None, "chip", None))
    return jax.shard_map(
        local,
        mesh=mesh,
        in_specs=placed,
        out_specs=(P(("cuts", "chip"), None), P(None, ("cuts", "chip"), None)),
        check_vma=False,
    )
```

```python
import jax
import jax.numpy as jnp
import numpy as np
from jax import lax
from jax.experimental import pallas as pl
from jax.experimental.pallas import tpu as pltpu
from jax.sharding import PartitionSpec as P

MESH = pl.DeviceIdType.MESH
F32 = jnp.float32
BF16 = jnp.bfloat16

HD = 128
SEQ = 128
HALF = 2560
ITEM = 640
CHUNK = 1280
BLOCK = 160
UNITS = 80


def rope_tables():
    half = HD // 2
    rates = 10000.0 ** (-(np.arange(half) * 2.0) / HD)
    angle = np.arange(SEQ)[:, None] * rates[None, :]
    cosine, sine = np.cos(angle), np.sin(angle)
    return np.stack(
        [np.concatenate([cosine, cosine], axis=1), np.concatenate([-sine, sine], axis=1)]
    ).astype(np.float32)


def turn_table():
    order = np.arange(ITEM).reshape(2, 2, 8, 20).transpose(1, 2, 0, 3).reshape(-1)
    table = np.zeros((ITEM, ITEM), np.float32)
    table[np.arange(ITEM), order] = 1.0
    return table


def dot(a, b):
    return jnp.dot(a, b, preferred_element_type=F32)


def dot_nt(a, b):
    return lax.dot_general(a, b, (((1,), (1,)), ((), ())), preferred_element_type=F32)


def kernel(
    hid, og, wts, cs, turn, ig_out, wg_out,
    Hb, Ob, W, HT, HP, OT, CS, TN, acc, accr, DD,
    PX, Ropp, Rn, Ro, Sb, PY, PZ, RY, RZ, Dz, Dy, DxY, DxZ, SY, SZ, Ty, Tz, Uy, Uz, Fy, Fz, IG,
    loc_sem, sib_s, sib_r, g1_s, g1_r, b_s, b_r, cp_s, cp_r, c_s, c_r,
    opp_s, opp_r, nb_s, nb_r, own_s, own_r, ry_s, ry_r, rz_s, rz_r,
    dz_s, dz_r, dy_s, dy_r, dxy_s, dxy_r, dxz_s, dxz_r, fy_s, fy_r, fz_s, fz_r,
):
    ci = lax.axis_index("cuts")
    ch = lax.axis_index("chip")
    x = ci // 8
    zh = (ci // 2) % 4
    c = ci % 2
    y = ch // 2
    zl = ch % 2
    z = zh * 2 + zl
    o = 1 - c

    def dev(x_, y_, z_, c_):
        return (x_ * 8 + (z_ // 2) * 2 + c_, y_ * 2 + z_ % 2)

    def rcopy(src, dst, ss, rs, to):
        return pltpu.make_async_remote_copy(
            src_ref=src, dst_ref=dst, send_sem=ss, recv_sem=rs, device_id=to, device_id_type=MESH
        )

    def when(cond):
        return pl.when(cond)

    def unless(cond):
        return pl.when(jnp.logical_not(cond))

    def rows(start, size, step):
        return pl.ds(pl.multiple_of(start, step), size)

    sib = dev(x, y, z, o)
    yq = y % 4
    active = y // 4 == c
    mine = rows(c * SEQ, SEQ, SEQ)
    theirs = rows(o * SEQ, SEQ, SEQ)
    col_c = rows(c * HALF, HALF, HALF)
    col_o = rows(o * HALF, HALF, HALF)
    yp, ym = (y + 1) % 8, (y + 7) % 8
    zp, zm = (z + 1) % 8, (z + 7) % 8
    xp, xm = (x + 1) % 4, (x + 3) % 4

    lh = pltpu.make_async_copy(hid.at[:, col_c], Hb.at[mine, :], loc_sem.at[0])
    lo = pltpu.make_async_copy(og.at[:, col_c], Ob.at[mine, :], loc_sem.at[1])
    lw = pltpu.make_async_copy(
        wts.at[pl.ds(0, 2)], W.at[pl.ds(0, 2), yq, rows(zl * 320, 320, 64), :], loc_sem.at[2]
    )
    lq = pltpu.make_async_copy(
        wts.at[pl.ds(2, 2), rows(zh * UNITS, UNITS, 16), :],
        W.at[pl.ds(2, 2), yq, rows(zl * 320 + zh * UNITS, UNITS, 16), :],
        loc_sem.at[6],
    )
    lc = pltpu.make_async_copy(cs, CS, loc_sem.at[4])
    lt = pltpu.make_async_copy(turn, TN, loc_sem.at[5])

    @when(active)
    def _():
        lw.start()
        lq.start()

    lh.start()
    lo.start()
    lt.start()
    lc.start()

    bar = pltpu.get_barrier_semaphore()

    def greet(to):
        pl.semaphore_signal(bar, inc=1, device_id=to, device_id_type=MESH)

    for dy in range(1, 8):
        for l in (0, 1):
            greet(dev(x, (y + dy) % 8, zh * 2 + l, c))
    for dz in range(1, 8):
        greet(dev(x, y, (z + dz) % 8, c))
    for dx in (1, 2, 3):
        for cc in (0, 1):
            greet(dev((x + dx) % 4, y, z, cc))
    greet(sib)
    acc[...] = jnp.zeros_like(acc)
    Ty[...] = jnp.zeros_like(Ty)
    Tz[...] = jnp.zeros_like(Tz)
    pl.semaphore_wait(bar, 14 + 7 + 6 + 1)

    def cp_copy(dy):
        at = rows(zh * UNITS, UNITS, 16)
        return rcopy(
            wts.at[pl.ds(2, 2), at, :],
            W.at[pl.ds(2, 2), yq, rows(zl * 320 + zh * UNITS, UNITS, 16), :],
            cp_s.at[dy], cp_r.at[yq], dev(x, (y + dy) % 8, z, c),
        )

    def g1_copy(i, l):
        return rcopy(
            wts.at[pl.ds(0, 2), pl.ds(160 * i, 160), :],
            W.at[pl.ds(0, 2), yq, rows(l * 320 + 160 * i, 160, 32), :],
            g1_s.at[i], g1_r.at[i], dev(x, y, (zp, zm)[i], c),
        )

    @when(active)
    def _():
        g1_copy(0, zl).start()
        g1_copy(1, zl).start()
        for dy in (1, 7, 2, 6, 3, 5, 4):
            cp_copy(dy).start()

    sh = rcopy(hid.at[:, col_o], Hb.at[mine, :], sib_s.at[0], sib_r.at[0], sib)
    so = rcopy(og.at[:, col_o], Ob.at[mine, :], sib_s.at[1], sib_r.at[1], sib)
    sh.start()
    so.start()

    def b_copy(s, t, d, sub):
        r = W.at[sub, s % 4]
        return rcopy(r, r, b_s.at[t, d, sub], b_r.at[s % 4, sub], dev(x, (yp, ym)[d], z, c))

    def c_copy(s, t, d, sub):
        r = W.at[2 + sub, :, rows((s % 2) * 320 + (s // 2) * UNITS, UNITS, 16), :]
        return rcopy(r, r, c_s.at[t, d, sub], c_r.at[s, sub], dev(x, y, (zp, zm)[d], c))

    def project_qk(s):
        at = rows((s % 4) * ITEM, ITEM, 128)
        acc[:, 0:256] += dot(Hb[:, at], jnp.concatenate([W[0, s % 4], W[1, s % 4]], axis=1))

    def transpose(src, dst, q):
        turned = src[:, q * ITEM : (q + 1) * ITEM].T
        for i in range(4):
            zr, cr = (q % 2) * 2 + i // 2, i % 2
            at = (q // 2) * CHUNK + (cr * 4 + zr) * BLOCK
            dst[at : at + BLOCK, :] = turned[i * BLOCK : (i + 1) * BLOCK, :]

    def transpose_turned(xr):
        low = dot_nt(TN[...], Hb[:, xr * CHUNK : xr * CHUNK + ITEM])
        high = dot_nt(TN[...], Hb[:, xr * CHUNK + ITEM : (xr + 1) * CHUNK])
        for g in range(16):
            at = xr * CHUNK + g * UNITS
            both = jnp.concatenate([low[g * 40 : g * 40 + 40], high[g * 40 : g * 40 + 40]], axis=0)
            HP[at : at + UNITS, :] = both.astype(BF16)

    order = ((0, 0), (1, 1), (1, 0), (0, 1))

    @when(active)
    def _():
        lw.wait()
        lq.wait()
        g1_copy(0, 1 - zl).wait_recv()
        g1_copy(1, 1 - zl).wait_recv()
        for sub, d in order:
            b_copy(y, 0, d, sub).start()

    for k in range(4):
        @unless(active & (k == yq))
        def _():
            at = rows(zl * 320 + zh * UNITS, UNITS, 16)
            r = W.at[pl.ds(2, 2), k, at, :]
            rcopy(r, r, cp_s.at[1], cp_r.at[k], dev(x, yp, z, c)).wait_recv()

    for sub, d in order:
        c_copy(z, 0, d, sub).start()

    lh.wait()
    sh.wait_recv()
    for q in range(4):
        transpose(Hb, HT, q)

    @when(active)
    def _():
        project_qk(y)

    for t in range(1, 5):
        ys = ((y + 8 - t) % 8, (y + t) % 8)
        zs = ((z + 8 - t) % 8, (z + t) % 8)
        if t < 4:
            for i in (0, 1):
                for d in (0, 1):
                    s = ys[d]
                    sub = i if d == 0 else 1 - i

                    @when(s // 4 == c)
                    def _():
                        b_copy(s, 0, 0, sub).wait_recv()
                        if t < 3 or sub == d:
                            b_copy(s, t, d, sub).start()

                for d in (0, 1):
                    s = zs[d]
                    sub = i if d == 0 else 1 - i
                    c_copy(s, 0, 0, sub).wait_recv()
                    if t < 3 or sub == d:
                        c_copy(s, t, d, sub).start()

            if t == 1:
                lt.wait()
                transpose_turned(0)
                transpose_turned(1)
            if t == 2:
                lo.wait()
                so.wait_recv()
                for q in range(4):
                    transpose(Ob, OT, q)
            for d in (0, 1):
                s = ys[d]

                @when(s // 4 == c)
                def _():
                    project_qk(s)

        else:
            s = ys[0]

            @when(s // 4 == c)
            def _():
                b_copy(s, 0, 0, 0).wait_recv()
                b_copy(s, 0, 0, 1).wait_recv()
                project_qk(s)

            c_copy(zs[0], 0, 0, 0).wait_recv()
            c_copy(zs[0], 0, 0, 1).wait_recv()

    wv = jnp.concatenate([W[2, k] for k in range(4)], axis=0)
    acc[:, 256:384] = dot(Hb[...], wv)
    wo = jnp.concatenate([W[3, k] for k in range(4)], axis=0)
    acc[:, 384:512] = dot(Ob[...], wo)

    sa = rcopy(acc.at[theirs, :], accr, sib_s.at[2], sib_r.at[2], sib)
    sa.start()
    lc.wait()
    cosine, sine = CS[0], CS[1]

    def rope(v, sgn):
        return v * cosine + pltpu.roll(v, 64, 1) * (sine * sgn)

    scale = 1.0 / np.sqrt(np.float32(HD))
    at_row = lax.broadcasted_iota(jnp.int32, (SEQ, SEQ), 0)
    at_col = lax.broadcasted_iota(jnp.int32, (SEQ, SEQ), 1)
    sa.wait_recv()
    summed = acc[mine, :] + accr[...]
    query = rope(summed[:, 0:128], 1.0).astype(BF16)
    keys = rope(summed[:, 128:256], 1.0).astype(BF16)
    values = summed[:, 256:384].astype(BF16)
    d_attn = summed[:, 384:512].astype(BF16)
    scores = dot_nt(query, keys) * scale
    d_prob = dot_nt(d_attn, values)
    scores = jnp.where(at_col <= at_row, scores, -jnp.inf)
    expo = jnp.exp(scores - jnp.max(scores, axis=1, keepdims=True))
    prob = expo / jnp.sum(expo, axis=1, keepdims=True)
    prob_b = prob.astype(BF16)
    attn = dot(prob_b, values)
    d_score = prob * (d_prob - jnp.sum(prob * d_prob, axis=1, keepdims=True)) * scale
    d_query = rope(dot(d_score.astype(BF16), keys), -1.0)
    d_key = rope(dot(d_score.T.astype(BF16), query), -1.0)
    d_value = dot(prob.T.astype(BF16), d_attn)
    DD[mine, :] = jnp.concatenate([d_query, d_key, d_value, attn], axis=1).astype(BF16)
    sd = rcopy(DD.at[mine, :], DD.at[mine, :], sib_s.at[3], sib_r.at[3], sib)
    sd.start()
    rcopy(DD.at[theirs, :], DD.at[theirs, :], sib_s.at[3], sib_r.at[3], sib).wait_recv()

    dd = (2 * c + 4 - x) % 4
    is_opp = (dd == 1) | (dd == 2)
    plus = dd < 2
    kn = jnp.where((dd == 0) | (dd == 2), 1, 0)
    ks = 1 - kn
    xn = jnp.where(plus, xp, xm)
    slot = jnp.where(plus, 0, 1)
    half_f = jnp.where(plus, 0, 1)
    half_d = 1 - half_f

    def lane(h):
        return pl.ds(pl.multiple_of(h * 128, 128), 128)

    def x_piece(k, rb):
        at = rows(k * CHUNK + rb * BLOCK, BLOCK, 32)
        left = dot(HT[at, :], DD[:, 0:128])
        right = dot(HP[at, :], DD[:, 128:256])
        return jnp.concatenate([left, right], axis=1).astype(BF16)

    def opp_copy(rb, h):
        return rcopy(
            PX.at[rows(ks * CHUNK + rb * BLOCK, BLOCK, 32), lane(h)],
            Ropp.at[rows(rb * BLOCK, BLOCK, 32), :],
            opp_s.at[rb, h], opp_r.at[rb], dev((xp, xm)[h], y, z, c),
        )

    def nb_copy(rb, h):
        cr, zr = rb // 4, rb % 4
        return rcopy(
            PX.at[rows(kn * CHUNK + rb * BLOCK, BLOCK, 32), lane(h)],
            Rn.at[slot, rows(zr * BLOCK, BLOCK, 32), lane(h)],
            nb_s.at[rb, h], nb_r.at[slot, zr, h], dev(xn, y, z, cr),
        )

    def own_copy(zr):
        return rcopy(
            PX.at[rows(ks * CHUNK + (o * 4 + zr) * BLOCK, BLOCK, 32), :],
            Ro.at[rows(zr * BLOCK, BLOCK, 32), :],
            own_s.at[zr], own_r.at[zr], sib,
        )

    def ring(pos, mat, lanes, PR, RR, s_sem, r_sem, to):
        def chunk_of(k, d):
            return (pos + (k if d == 0 else 8 - k)) % 8

        def compute(i):
            lhs = jnp.concatenate(
                [mat[rows(g * 640 + i * UNITS, UNITS, 16), :] for g in range(4)], axis=0
            )
            PR[i] = dot(lhs, DD[:, lanes : lanes + 128]).astype(BF16)

        def copy(k, d):
            i = chunk_of(k, d)
            at = pl.ds(160 * d, 160) if k == 4 else pl.ds(0, 320)
            return rcopy(
                PR.at[i, at, :], RR.at[d, k - 1, at, :], s_sem.at[k - 1, d], r_sem.at[k - 1, d], to[d]
            )

        def step(k):
            for d in (0, 1):
                i = chunk_of(k, d)
                if k == 3:
                    copy(4, d).wait_recv()
                    at = slice(160 * d, 160 * d + 160)
                    PR[i, at, :] = (PR[i, at, :].astype(F32) + RR[d, 3, at, :].astype(F32)).astype(BF16)
                elif k < 3:
                    copy(k + 1, d).wait_recv()
                    PR[i] = (PR[i].astype(F32) + RR[d, k].astype(F32)).astype(BF16)
                copy(k, d).start()

        def finish():
            copy(1, 0).wait_recv()
            copy(1, 1).wait_recv()
            return PR[pos].astype(F32) + RR[0, 0].astype(F32) + RR[1, 0].astype(F32)

        def wait_sends():
            for k in range(1, 5):
                for d in (0, 1):
                    copy(k, d).wait_send()

        def compute_for(k):
            compute(chunk_of(k, 0))
            if k not in (0, 4):
                compute(chunk_of(k, 1))

        return compute_for, step, finish, wait_sends

    y_ring = ring(y, HP, 256, PY, RY, ry_s, ry_r, (dev(x, yp, z, c), dev(x, ym, z, c)))
    z_ring = ring(z, OT, 384, PZ, RZ, rz_s, rz_r, (dev(x, y, zp, c), dev(x, y, zm, c)))

    def dx_copy(S, R, a, cr, s_sem, r_sem):
        return rcopy(
            S.at[pl.ds((a * 2 + cr) * UNITS, UNITS), :], R.at[x],
            s_sem.at[a * 2 + cr], r_sem.at[x], dev(2 * c + a, y, z, cr),
        )

    def dx_send(S, R, s_sem, r_sem):
        for a in (0, 1):
            for cr in (0, 1):
                to_self = (2 * c + a == x) & (cr == c)

                @when(to_self)
                def _():
                    R[x] = S[(a * 2 + cr) * UNITS : (a * 2 + cr + 1) * UNITS, :]

                @unless(to_self)
                def _():
                    dx_copy(S, R, a, cr, s_sem, r_sem).start()

    def dx_receive(R, s_sem, r_sem):
        total = None
        for k in range(4):
            @unless((k == x) & (x // 2 == c))
            def _():
                rcopy(R.at[k], R.at[k], s_sem.at[0], r_sem.at[k], sib).wait_recv()

            total = R[k].astype(F32) if total is None else total + R[k].astype(F32)
        return total

    def dx_wait(S, R, s_sem, r_sem):
        for a in (0, 1):
            for cr in (0, 1):
                @unless((2 * c + a == x) & (cr == c))
                def _():
                    dx_copy(S, R, a, cr, s_sem, r_sem).wait_send()

    def dz_copy(i):
        return rcopy(
            Sb.at[rows(i * UNITS, UNITS, 16), pl.ds(0, 128)], Dz.at[z],
            dz_s.at[i], dz_r.at[z], dev(x, y, i, c),
        )

    def dy_copy(i):
        return rcopy(
            Sb.at[rows(i * UNITS, UNITS, 16), pl.ds(128, 128)], Dy.at[y],
            dy_s.at[i], dy_r.at[y], dev(x, i, z, c),
        )

    def fy_copy(k):
        yr, lr = zl * 4 + k // 2, k % 2
        return rcopy(Uy.at[k], Fy.at[y], fy_s.at[k], fy_r.at[y], dev(x, yr, zh * 2 + lr, c))

    def fz_copy(k):
        return rcopy(Uz.at[k], Fz.at[z], fz_s.at[k], fz_r.at[z], dev(x, y, k, c))

    self_k = yq * 2 + zl
    feeds_self = zl == y // 4

    y_ring[0](4)
    y_ring[1](4)
    z_ring[0](4)
    z_ring[1](4)

    @when(is_opp)
    def _():
        @pl.loop(0, 8)
        def _(rb):
            PX[rows(ks * CHUNK + rb * BLOCK, BLOCK, 32), :] = x_piece(ks, rb)
            opp_copy(rb, 0).start()
            opp_copy(rb, 1).start()

    @unless(is_opp)
    def _():
        @pl.loop(0, 8)
        def _(rb):
            PX[rows(kn * CHUNK + rb * BLOCK, BLOCK, 32), :] = x_piece(kn, rb)
            nb_copy(rb, half_d).start()

    y_ring[0](3)
    y_ring[1](3)
    z_ring[0](3)
    z_ring[1](3)

    @when(is_opp)
    def _():
        @pl.loop(0, 8)
        def _(rb):
            PX[rows(kn * CHUNK + rb * BLOCK, BLOCK, 32), :] = x_piece(kn, rb)
            nb_copy(rb, half_d).start()

    y_ring[0](2)
    y_ring[1](2)
    z_ring[0](2)
    z_ring[1](2)

    @pl.loop(0, 8)
    def _(rb):
        opp_copy(rb, 0).wait_recv()
        at = rows(kn * CHUNK + rb * BLOCK, BLOCK, 32)
        got = Ropp[rows(rb * BLOCK, BLOCK, 32), :]
        PX[at, lane(half_f)] = (PX[at, lane(half_f)].astype(F32) + got.astype(F32)).astype(BF16)
        nb_copy(rb, half_f).start()

    y_ring[0](1)
    y_ring[1](1)
    z_ring[0](1)
    z_ring[1](1)

    @unless(is_opp)
    def _():
        @pl.loop(0, 4)
        def _(zr):
            PX[rows(ks * CHUNK + (o * 4 + zr) * BLOCK, BLOCK, 32), :] = x_piece(ks, o * 4 + zr)
            own_copy(zr).start()

        @pl.loop(0, 4)
        def _(zr):
            Ro[rows(zr * BLOCK, BLOCK, 32), :] = x_piece(ks, c * 4 + zr)

    y_ring[0](0)
    z_ring[0](0)

    @pl.loop(0, 4)
    def _(q):
        wq = jnp.concatenate([W[0, q], W[1, q], W[2, q]], axis=1)
        IG[:, rows(q * ITEM, ITEM, 128)] = dot_nt(DD[:, 0:384], wq).astype(BF16)

    li = pltpu.make_async_copy(IG.at[mine, :], ig_out.at[:, col_c], loc_sem.at[3])
    li.start()
    si = rcopy(IG.at[theirs, :], ig_out.at[:, col_c], sib_s.at[4], sib_r.at[4], sib)
    si.start()

    SY[...] = y_ring[2]().astype(BF16)
    dx_send(SY, DxY, dxy_s, dxy_r)
    SZ[...] = z_ring[2]().astype(BF16)
    dx_send(SZ, DxZ, dxz_s, dxz_r)

    @pl.loop(0, 4)
    def _(zr):
        at = rows(zr * BLOCK, BLOCK, 32)

        @when(is_opp)
        def _():
            own_copy(zr).wait_recv()

        for src in (0, 1):
            for h in (0, 1):
                r = Rn.at[src, at, pl.ds(128 * h, 128)]
                rcopy(r, r, nb_s.at[0, 0], nb_r.at[src, zr, h], sib).wait_recv()
        total = Ro[at, :].astype(F32) + Rn[0, at, :].astype(F32) + Rn[1, at, :].astype(F32)
        Sb[at, :] = total.astype(BF16)
        for s in (0, 1):
            i = zr * 2 + s

            @when(i != z)
            def _():
                dz_copy(i).start()

            @when(i != y)
            def _():
                dy_copy(i).start()

    Dz[z] = Sb[rows(z * UNITS, UNITS, 16), 0:128]
    Dy[y] = Sb[rows(y * UNITS, UNITS, 16), 128:256]
    Ty[0:UNITS, 128:256] = dx_receive(DxZ, dxz_s, dxz_r)
    Tz[0:UNITS, 128:256] = dx_receive(DxY, dxy_s, dxy_r)

    @pl.loop(0, 8)
    def _(k):
        @when(k != z)
        def _():
            rcopy(Dz.at[k], Dz.at[k], dz_s.at[k], dz_r.at[k], dev(x, y, k, c)).wait_recv()

        Ty[0:UNITS, 0:128] = Ty[0:UNITS, 0:128] + Dz[k].astype(F32)

    for k in range(8):
        unit = Ty[10 * k : 10 * k + 16, :].astype(BF16)
        Uy[k] = unit
        to_self = feeds_self & (self_k == k)

        @when(to_self)
        def _():
            Fy[y] = unit

        @unless(to_self)
        def _():
            fy_copy(k).start()

    @pl.loop(0, 8)
    def _(k):
        @when(k != y)
        def _():
            rcopy(Dy.at[k], Dy.at[k], dy_s.at[k], dy_r.at[k], dev(x, k, z, c)).wait_recv()

        Tz[0:UNITS, 0:128] = Tz[0:UNITS, 0:128] + Dy[k].astype(F32)

    for k in range(8):
        unit = Tz[10 * k : 10 * k + 16, :].astype(BF16)
        Uz[k] = unit

        @when(k == z)
        def _():
            Fz[z] = unit

        @when(k != z)
        def _():
            fz_copy(k).start()

    total = None
    for k in range(8):
        @unless(feeds_self & (y == k))
        def _():
            rcopy(Fy.at[k], Fy.at[k], fy_s.at[k], fy_r.at[k], sib).wait_recv()

        total = Fy[k].astype(F32) if total is None else total + Fy[k].astype(F32)
    total = total * (1.0 / 512.0)
    wg_out[0] = total[0:10, 0:128]
    wg_out[3] = total[0:10, 128:256]
    total = None
    for k in range(8):
        @when(z != k)
        def _():
            rcopy(Fz.at[k], Fz.at[k], fz_s.at[k], fz_r.at[k], sib).wait_recv()

        total = Fz[k].astype(F32) if total is None else total + Fz[k].astype(F32)
    total = total * (1.0 / 512.0)
    wg_out[1] = total[0:10, 0:128]
    wg_out[2] = total[0:10, 128:256]

    sh.wait_send()
    so.wait_send()

    @when(active)
    def _():
        g1_copy(0, zl).wait_send()
        g1_copy(1, zl).wait_send()
        for dy in range(1, 8):
            cp_copy(dy).wait_send()
        for sub, d in order:
            b_copy(y, 0, d, sub).wait_send()

    for sub, d in order:
        c_copy(z, 0, d, sub).wait_send()
    for t in range(1, 4):
        for d in (0, 1):
            s = ((y + 8 - t) % 8, (y + t) % 8)[d]
            zs = ((z + 8 - t) % 8, (z + t) % 8)[d]
            for sub in (0, 1):
                if t < 3 or sub == d:
                    c_copy(zs, t, d, sub).wait_send()

                    @when(s // 4 == c)
                    def _():
                        b_copy(s, t, d, sub).wait_send()

    sa.wait_send()
    sd.wait_send()

    li.wait()
    si.wait()
    y_ring[3]()
    z_ring[3]()
    dx_wait(SY, DxY, dxy_s, dxy_r)
    dx_wait(SZ, DxZ, dxz_s, dxz_r)

    @pl.loop(0, 8)
    def _(k):
        nb_copy(k, half_f).wait_send()
        nb_copy(k, half_d).wait_send()

        @when(is_opp)
        def _():
            opp_copy(k, 0).wait_send()
            opp_copy(k, 1).wait_send()

        @when(k != z)
        def _():
            dz_copy(k).wait_send()

        @when(k != y)
        def _():
            dy_copy(k).wait_send()

    @unless(is_opp)
    def _():
        @pl.loop(0, 4)
        def _(zr):
            own_copy(zr).wait_send()

    @pl.loop(0, 8)
    def _(k):
        @when(k != z)
        def _():
            fz_copy(k).wait_send()

        @unless(feeds_self & (self_k == k))
        def _():
            fy_copy(k).wait_send()


def local(hidden, out_grad, weights):
    table = jnp.asarray(rope_tables())
    turn = jnp.asarray(turn_table(), BF16)
    vmem = pl.BlockSpec(memory_space=pltpu.VMEM)
    hbm = pl.BlockSpec(memory_space=pltpu.HBM)
    dma = pltpu.SemaphoreType.DMA
    v = pltpu.VMEM
    return pl.pallas_call(
        kernel,
        out_shape=(
            jax.ShapeDtypeStruct(hidden.shape, BF16),
            jax.ShapeDtypeStruct((4, 10, HD), F32),
        ),
        in_specs=[hbm] * 5,
        out_specs=(hbm, vmem),
        scratch_shapes=[
            v((256, HALF), BF16),
            v((256, HALF), BF16),
            v((4, 4, ITEM, HD), BF16),
            v((HALF, 256), BF16),
            v((HALF, 256), BF16),
            v((HALF, 256), BF16),
            v((2, SEQ, HD), F32),
            v((ITEM, ITEM), BF16),
            v((256, 512), F32),
            v((SEQ, 512), F32),
            v((256, 512), BF16),
            v((HALF, 256), BF16),
            v((CHUNK, 128), BF16),
            v((2, 640, 256), BF16),
            v((640, 256), BF16),
            v((640, 256), BF16),
            v((8, 320, 128), BF16),
            v((8, 320, 128), BF16),
            v((2, 4, 320, 128), BF16),
            v((2, 4, 320, 128), BF16),
            v((8, UNITS, 128), BF16),
            v((8, UNITS, 128), BF16),
            v((4, UNITS, 128), BF16),
            v((4, UNITS, 128), BF16),
            v((320, 128), BF16),
            v((320, 128), BF16),
            v((96, 256), F32),
            v((96, 256), F32),
            v((8, 16, 256), BF16),
            v((8, 16, 256), BF16),
            v((8, 16, 256), BF16),
            v((8, 16, 256), BF16),
            v((256, HALF), BF16),
            dma((7,)), dma((5,)), dma((5,)),
            dma((2,)), dma((2,)),
            dma((4, 2, 2)), dma((4, 2)),
            dma((8,)), dma((4,)),
            dma((4, 2, 2)), dma((8, 2)),
            dma((8, 2)), dma((8,)),
            dma((8, 2)), dma((2, 4, 2)),
            dma((4,)), dma((4,)),
            dma((4, 2)), dma((4, 2)),
            dma((4, 2)), dma((4, 2)),
            dma((8,)), dma((8,)),
            dma((8,)), dma((8,)),
            dma((4,)), dma((4,)),
            dma((4,)), dma((4,)),
            dma((8,)), dma((8,)),
            dma((8,)), dma((8,)),
        ],
        compiler_params=pltpu.CompilerParams(
            collective_id=0, has_side_effects=True, vmem_limit_bytes=62 * 1024 * 1024
        ),
    )(hidden, out_grad, weights, table, turn)


def solution(mesh):
    placed = (P(("cuts", "chip"), None), P(("cuts", "chip"), None), P(None, "chip", None))
    return jax.shard_map(
        local,
        mesh=mesh,
        in_specs=placed,
        out_specs=(P(("cuts", "chip"), None), P(None, ("cuts", "chip"), None)),
        check_vma=False,
    )
```

```python
import jax
import jax.numpy as jnp
import numpy as np
from jax import lax
from jax.experimental import pallas as pl
from jax.experimental.pallas import tpu as pltpu
from jax.sharding import PartitionSpec as P

MESH = pl.DeviceIdType.MESH
F32 = jnp.float32
BF16 = jnp.bfloat16

HD = 128
SEQ = 128
HALF = 2560
ITEM = 640
CHUNK = 1280
BLOCK = 160
UNITS = 80


def rope_tables():
    half = HD // 2
    rates = 10000.0 ** (-(np.arange(half) * 2.0) / HD)
    angle = np.arange(SEQ)[:, None] * rates[None, :]
    cosine, sine = np.cos(angle), np.sin(angle)
    return np.stack(
        [np.concatenate([cosine, cosine], axis=1), np.concatenate([-sine, sine], axis=1)]
    ).astype(np.float32)


def turn_table():
    order = np.arange(ITEM).reshape(2, 2, 8, 20).transpose(1, 2, 0, 3).reshape(-1)
    table = np.zeros((ITEM, ITEM), np.float32)
    table[np.arange(ITEM), order] = 1.0
    return table


def dot(a, b):
    return jnp.dot(a, b, preferred_element_type=F32)


def dot_nt(a, b):
    return lax.dot_general(a, b, (((1,), (1,)), ((), ())), preferred_element_type=F32)


def kernel(
    hid, og, wts, cs, turn, ig_out, wg_out,
    Hb, Ob, W, HT, HP, OT, CS, TN, acc, accr, DD,
    PX, Ropp, Rn, Ro, Sb, PY, PZ, RY, RZ, Dz, Dy, DxY, DxZ, SY, SZ, Ty, Tz, Uy, Uz, Fy, Fz, IG,
    loc_sem, sib_s, sib_r, g1_s, g1_r, b_s, b_r, cp_s, cp_r, c_s, c_r,
    opp_s, opp_r, nb_s, nb_r, own_s, own_r, ry_s, ry_r, rz_s, rz_r,
    dz_s, dz_r, dy_s, dy_r, dxy_s, dxy_r, dxz_s, dxz_r, fy_s, fy_r, fz_s, fz_r,
):
    ci = lax.axis_index("cuts")
    ch = lax.axis_index("chip")
    x = ci // 8
    zh = (ci // 2) % 4
    c = ci % 2
    y = ch // 2
    zl = ch % 2
    z = zh * 2 + zl
    o = 1 - c

    def dev(x_, y_, z_, c_):
        return (x_ * 8 + (z_ // 2) * 2 + c_, y_ * 2 + z_ % 2)

    def rcopy(src, dst, ss, rs, to):
        return pltpu.make_async_remote_copy(
            src_ref=src, dst_ref=dst, send_sem=ss, recv_sem=rs, device_id=to, device_id_type=MESH
        )

    def when(cond):
        return pl.when(cond)

    def unless(cond):
        return pl.when(jnp.logical_not(cond))

    def rows(start, size, step):
        return pl.ds(pl.multiple_of(start, step), size)

    sib = dev(x, y, z, o)
    yq = y % 4
    active = y // 4 == c
    mine = rows(c * SEQ, SEQ, SEQ)
    theirs = rows(o * SEQ, SEQ, SEQ)
    col_c = rows(c * HALF, HALF, HALF)
    col_o = rows(o * HALF, HALF, HALF)
    yp, ym = (y + 1) % 8, (y + 7) % 8
    zp, zm = (z + 1) % 8, (z + 7) % 8
    xp, xm = (x + 1) % 4, (x + 3) % 4

    lh = pltpu.make_async_copy(hid.at[:, col_c], Hb.at[mine, :], loc_sem.at[0])
    lo = pltpu.make_async_copy(og.at[:, col_c], Ob.at[mine, :], loc_sem.at[1])
    lw = pltpu.make_async_copy(
        wts.at[pl.ds(0, 2)], W.at[pl.ds(0, 2), yq, rows(zl * 320, 320, 64), :], loc_sem.at[2]
    )
    lq = pltpu.make_async_copy(
        wts.at[pl.ds(2, 2), rows(zh * UNITS, UNITS, 16), :],
        W.at[pl.ds(2, 2), yq, rows(zl * 320 + zh * UNITS, UNITS, 16), :],
        loc_sem.at[6],
    )
    lc = pltpu.make_async_copy(cs, CS, loc_sem.at[4])
    lt = pltpu.make_async_copy(turn, TN, loc_sem.at[5])

    @when(active)
    def _():
        lw.start()
        lq.start()

    lh.start()
    lo.start()
    lt.start()
    lc.start()

    bar = pltpu.get_barrier_semaphore()

    def greet(to):
        pl.semaphore_signal(bar, inc=1, device_id=to, device_id_type=MESH)

    for dy in range(1, 8):
        for l in (0, 1):
            greet(dev(x, (y + dy) % 8, zh * 2 + l, c))
    for dz in range(1, 8):
        greet(dev(x, y, (z + dz) % 8, c))
    for dx in (1, 2, 3):
        for cc in (0, 1):
            greet(dev((x + dx) % 4, y, z, cc))
    greet(sib)
    acc[...] = jnp.zeros_like(acc)
    Ty[...] = jnp.zeros_like(Ty)
    Tz[...] = jnp.zeros_like(Tz)
    pl.semaphore_wait(bar, 14 + 7 + 6 + 1)

    def cp_copy(dy):
        at = rows(zh * UNITS, UNITS, 16)
        return rcopy(
            wts.at[pl.ds(2, 2), at, :],
            W.at[pl.ds(2, 2), yq, rows(zl * 320 + zh * UNITS, UNITS, 16), :],
            cp_s.at[dy], cp_r.at[yq], dev(x, (y + dy) % 8, z, c),
        )

    def g1_copy(i, l):
        return rcopy(
            wts.at[pl.ds(0, 2), pl.ds(160 * i, 160), :],
            W.at[pl.ds(0, 2), yq, rows(l * 320 + 160 * i, 160, 32), :],
            g1_s.at[i], g1_r.at[i], dev(x, y, (zp, zm)[i], c),
        )

    @when(active)
    def _():
        g1_copy(0, zl).start()
        g1_copy(1, zl).start()
        for dy in (1, 7, 2, 6, 3, 5, 4):
            cp_copy(dy).start()

    sh = rcopy(hid.at[:, col_o], Hb.at[mine, :], sib_s.at[0], sib_r.at[0], sib)
    so = rcopy(og.at[:, col_o], Ob.at[mine, :], sib_s.at[1], sib_r.at[1], sib)
    sh.start()
    so.start()

    def b_copy(s, t, d, sub):
        r = W.at[sub, s % 4]
        return rcopy(r, r, b_s.at[t, d, sub], b_r.at[s % 4, sub], dev(x, (yp, ym)[d], z, c))

    def c_copy(s, t, d, sub):
        r = W.at[2 + sub, :, rows((s % 2) * 320 + (s // 2) * UNITS, UNITS, 16), :]
        return rcopy(r, r, c_s.at[t, d, sub], c_r.at[s, sub], dev(x, y, (zp, zm)[d], c))

    def project_qk(s):
        at = rows((s % 4) * ITEM, ITEM, 128)
        acc[:, 0:256] += dot(Hb[:, at], jnp.concatenate([W[0, s % 4], W[1, s % 4]], axis=1))

    def transpose(src, dst, q):
        turned = src[:, q * ITEM : (q + 1) * ITEM].T
        for i in range(4):
            zr, cr = (q % 2) * 2 + i // 2, i % 2
            at = (q // 2) * CHUNK + (cr * 4 + zr) * BLOCK
            dst[at : at + BLOCK, :] = turned[i * BLOCK : (i + 1) * BLOCK, :]

    def transpose_turned(xr):
        low = dot_nt(TN[...], Hb[:, xr * CHUNK : xr * CHUNK + ITEM])
        high = dot_nt(TN[...], Hb[:, xr * CHUNK + ITEM : (xr + 1) * CHUNK])
        for g in range(16):
            at = xr * CHUNK + g * UNITS
            both = jnp.concatenate([low[g * 40 : g * 40 + 40], high[g * 40 : g * 40 + 40]], axis=0)
            HP[at : at + UNITS, :] = both.astype(BF16)

    order = ((0, 0), (1, 1), (1, 0), (0, 1))

    @when(active)
    def _():
        lw.wait()
        lq.wait()
        g1_copy(0, 1 - zl).wait_recv()
        g1_copy(1, 1 - zl).wait_recv()
        for sub, d in order:
            b_copy(y, 0, d, sub).start()

    for k in range(4):
        @unless(active & (k == yq))
        def _():
            at = rows(zl * 320 + zh * UNITS, UNITS, 16)
            r = W.at[pl.ds(2, 2), k, at, :]
            rcopy(r, r, cp_s.at[1], cp_r.at[k], dev(x, yp, z, c)).wait_recv()

    for sub, d in order:
        c_copy(z, 0, d, sub).start()

    lh.wait()
    sh.wait_recv()
    for q in range(4):
        transpose(Hb, HT, q)

    @when(active)
    def _():
        project_qk(y)

    for t in range(1, 5):
        ys = ((y + 8 - t) % 8, (y + t) % 8)
        zs = ((z + 8 - t) % 8, (z + t) % 8)
        if t < 4:
            for i in (0, 1):
                for d in (0, 1):
                    s = ys[d]
                    sub = i if d == 0 else 1 - i

                    @when(s // 4 == c)
                    def _():
                        b_copy(s, 0, 0, sub).wait_recv()
                        if t < 3 or sub == d:
                            b_copy(s, t, d, sub).start()

                for d in (0, 1):
                    s = zs[d]
                    sub = i if d == 0 else 1 - i
                    c_copy(s, 0, 0, sub).wait_recv()
                    if t < 3 or sub == d:
                        c_copy(s, t, d, sub).start()

            if t == 1:
                lt.wait()
                transpose_turned(0)
                transpose_turned(1)
            if t == 2:
                lo.wait()
                so.wait_recv()
                for q in range(4):
                    transpose(Ob, OT, q)
            for d in (0, 1):
                s = ys[d]

                @when(s // 4 == c)
                def _():
                    project_qk(s)

        else:
            s = ys[0]

            @when(s // 4 == c)
            def _():
                b_copy(s, 0, 0, 0).wait_recv()
                b_copy(s, 0, 0, 1).wait_recv()
                project_qk(s)

            c_copy(zs[0], 0, 0, 0).wait_recv()
            c_copy(zs[0], 0, 0, 1).wait_recv()

    wv = jnp.concatenate([W[2, k] for k in range(4)], axis=0)
    acc[:, 256:384] = dot(Hb[...], wv)
    wo = jnp.concatenate([W[3, k] for k in range(4)], axis=0)
    acc[:, 384:512] = dot(Ob[...], wo)

    sa = rcopy(acc.at[theirs, :], accr, sib_s.at[2], sib_r.at[2], sib)
    sa.start()
    lc.wait()
    cosine, sine = CS[0], CS[1]

    def rope(v, sgn):
        return v * cosine + pltpu.roll(v, 64, 1) * (sine * sgn)

    scale = 1.0 / np.sqrt(np.float32(HD))
    at_row = lax.broadcasted_iota(jnp.int32, (SEQ, SEQ), 0)
    at_col = lax.broadcasted_iota(jnp.int32, (SEQ, SEQ), 1)
    sa.wait_recv()
    summed = acc[mine, :] + accr[...]
    query = rope(summed[:, 0:128], 1.0).astype(BF16)
    keys = rope(summed[:, 128:256], 1.0).astype(BF16)
    values = summed[:, 256:384].astype(BF16)
    d_attn = summed[:, 384:512].astype(BF16)
    scores = dot_nt(query, keys) * scale
    d_prob = dot_nt(d_attn, values)
    scores = jnp.where(at_col <= at_row, scores, -jnp.inf)
    expo = jnp.exp(scores - jnp.max(scores, axis=1, keepdims=True))
    prob = expo / jnp.sum(expo, axis=1, keepdims=True)
    prob_b = prob.astype(BF16)
    attn = dot(prob_b, values)
    d_score = prob * (d_prob - jnp.sum(prob * d_prob, axis=1, keepdims=True)) * scale
    d_query = rope(dot(d_score.astype(BF16), keys), -1.0)
    d_key = rope(dot(d_score.T.astype(BF16), query), -1.0)
    d_value = dot(prob.T.astype(BF16), d_attn)
    DD[mine, :] = jnp.concatenate([d_query, d_key, d_value, attn], axis=1).astype(BF16)
    sd = rcopy(DD.at[mine, :], DD.at[mine, :], sib_s.at[3], sib_r.at[3], sib)
    sd.start()
    rcopy(DD.at[theirs, :], DD.at[theirs, :], sib_s.at[3], sib_r.at[3], sib).wait_recv()

    dd = (2 * c + 4 - x) % 4
    is_opp = (dd == 1) | (dd == 2)
    plus = dd < 2
    kn = jnp.where((dd == 0) | (dd == 2), 1, 0)
    ks = 1 - kn
    xn = jnp.where(plus, xp, xm)
    slot = jnp.where(plus, 0, 1)
    half_f = jnp.where(plus, 0, 1)
    half_d = 1 - half_f

    def lane(h):
        return pl.ds(pl.multiple_of(h * 128, 128), 128)

    def x_piece(k, rb):
        at = rows(k * CHUNK + rb * BLOCK, BLOCK, 32)
        left = dot(HT[at, :], DD[:, 0:128])
        right = dot(HP[at, :], DD[:, 128:256])
        return jnp.concatenate([left, right], axis=1).astype(BF16)

    def opp_copy(rb, h):
        return rcopy(
            PX.at[rows(ks * CHUNK + rb * BLOCK, BLOCK, 32), lane(h)],
            Ropp.at[rows(rb * BLOCK, BLOCK, 32), :],
            opp_s.at[rb, h], opp_r.at[rb], dev((xp, xm)[h], y, z, c),
        )

    def nb_copy(rb, h):
        cr, zr = rb // 4, rb % 4
        return rcopy(
            PX.at[rows(kn * CHUNK + rb * BLOCK, BLOCK, 32), lane(h)],
            Rn.at[slot, rows(zr * BLOCK, BLOCK, 32), lane(h)],
            nb_s.at[rb, h], nb_r.at[slot, zr, h], dev(xn, y, z, cr),
        )

    def own_copy(zr):
        return rcopy(
            PX.at[rows(ks * CHUNK + (o * 4 + zr) * BLOCK, BLOCK, 32), :],
            Ro.at[rows(zr * BLOCK, BLOCK, 32), :],
            own_s.at[zr], own_r.at[zr], sib,
        )

    def ring(pos, mat, lanes, PR, RR, s_sem, r_sem, to):
        def chunk_of(k, d):
            return (pos + (k if d == 0 else 8 - k)) % 8

        def compute(i):
            lhs = jnp.concatenate(
                [mat[rows(g * 640 + i * UNITS, UNITS, 16), :] for g in range(4)], axis=0
            )
            PR[i] = dot(lhs, DD[:, lanes : lanes + 128]).astype(BF16)

        def copy(k, d):
            i = chunk_of(k, d)
            at = pl.ds(160 * d, 160) if k == 4 else pl.ds(0, 320)
            return rcopy(
                PR.at[i, at, :], RR.at[d, k - 1, at, :], s_sem.at[k - 1, d], r_sem.at[k - 1, d], to[d]
            )

        def step(k):
            for d in (0, 1):
                i = chunk_of(k, d)
                if k == 3:
                    copy(4, d).wait_recv()
                    at = slice(160 * d, 160 * d + 160)
                    PR[i, at, :] = (PR[i, at, :].astype(F32) + RR[d, 3, at, :].astype(F32)).astype(BF16)
                elif k < 3:
                    copy(k + 1, d).wait_recv()
                    PR[i] = (PR[i].astype(F32) + RR[d, k].astype(F32)).astype(BF16)
                copy(k, d).start()

        def finish():
            copy(1, 0).wait_recv()
            copy(1, 1).wait_recv()
            return PR[pos].astype(F32) + RR[0, 0].astype(F32) + RR[1, 0].astype(F32)

        def wait_sends():
            for k in range(1, 5):
                for d in (0, 1):
                    copy(k, d).wait_send()

        def compute_for(k):
            compute(chunk_of(k, 0))
            if k not in (0, 4):
                compute(chunk_of(k, 1))

        return compute_for, step, finish, wait_sends

    y_ring = ring(y, HP, 256, PY, RY, ry_s, ry_r, (dev(x, yp, z, c), dev(x, ym, z, c)))
    z_ring = ring(z, OT, 384, PZ, RZ, rz_s, rz_r, (dev(x, y, zp, c), dev(x, y, zm, c)))

    def dx_copy(S, R, a, cr, s_sem, r_sem):
        return rcopy(
            S.at[pl.ds((a * 2 + cr) * UNITS, UNITS), :], R.at[x],
            s_sem.at[a * 2 + cr], r_sem.at[x], dev(2 * c + a, y, z, cr),
        )

    def dx_send(S, R, s_sem, r_sem):
        for a in (0, 1):
            for cr in (0, 1):
                to_self = (2 * c + a == x) & (cr == c)

                @when(to_self)
                def _():
                    R[x] = S[(a * 2 + cr) * UNITS : (a * 2 + cr + 1) * UNITS, :]

                @unless(to_self)
                def _():
                    dx_copy(S, R, a, cr, s_sem, r_sem).start()

    def dx_receive(R, s_sem, r_sem):
        total = None
        for k in range(4):
            @unless((k == x) & (x // 2 == c))
            def _():
                rcopy(R.at[k], R.at[k], s_sem.at[0], r_sem.at[k], sib).wait_recv()

            total = R[k].astype(F32) if total is None else total + R[k].astype(F32)
        return total

    def dx_wait(S, R, s_sem, r_sem):
        for a in (0, 1):
            for cr in (0, 1):
                @unless((2 * c + a == x) & (cr == c))
                def _():
                    dx_copy(S, R, a, cr, s_sem, r_sem).wait_send()

    def dz_copy(i):
        return rcopy(
            Sb.at[rows(i * UNITS, UNITS, 16), pl.ds(0, 128)], Dz.at[z],
            dz_s.at[i], dz_r.at[z], dev(x, y, i, c),
        )

    def dy_copy(i):
        return rcopy(
            Sb.at[rows(i * UNITS, UNITS, 16), pl.ds(128, 128)], Dy.at[y],
            dy_s.at[i], dy_r.at[y], dev(x, i, z, c),
        )

    def fy_copy(k):
        yr, lr = zl * 4 + k // 2, k % 2
        return rcopy(Uy.at[k], Fy.at[y], fy_s.at[k], fy_r.at[y], dev(x, yr, zh * 2 + lr, c))

    def fz_copy(k):
        return rcopy(Uz.at[k], Fz.at[z], fz_s.at[k], fz_r.at[z], dev(x, y, k, c))

    self_k = yq * 2 + zl
    feeds_self = zl == y // 4

    def at_turn(i):
        return (i % 2) * 4 + i // 2

    def neighbour_pieces():
        @pl.loop(0, 8)
        def _(i):
            rb = at_turn(i)
            PX[rows(kn * CHUNK + rb * BLOCK, BLOCK, 32), :] = x_piece(kn, rb)
            nb_copy(rb, half_d).start()

    y_ring[0](4)
    y_ring[1](4)
    z_ring[0](4)
    z_ring[1](4)

    @when(is_opp)
    def _():
        @pl.loop(0, 8)
        def _(i):
            rb = at_turn(i)
            PX[rows(ks * CHUNK + rb * BLOCK, BLOCK, 32), :] = x_piece(ks, rb)
            opp_copy(rb, 0).start()
            opp_copy(rb, 1).start()

    @unless(is_opp)
    def _():
        neighbour_pieces()

    y_ring[0](3)
    y_ring[1](3)
    z_ring[0](3)
    z_ring[1](3)

    @when(is_opp)
    def _():
        neighbour_pieces()

    @unless(is_opp)
    def _():
        @pl.loop(0, 4)
        def _(zr):
            PX[rows(ks * CHUNK + (o * 4 + zr) * BLOCK, BLOCK, 32), :] = x_piece(ks, o * 4 + zr)
            own_copy(zr).start()

        @pl.loop(0, 4)
        def _(zr):
            Ro[rows(zr * BLOCK, BLOCK, 32), :] = x_piece(ks, c * 4 + zr)

    y_ring[0](2)
    y_ring[1](2)
    z_ring[0](2)
    z_ring[1](2)

    @pl.loop(0, 4)
    def _(q):
        wq = jnp.concatenate([W[0, q], W[1, q], W[2, q]], axis=1)
        IG[:, rows(q * ITEM, ITEM, 128)] = dot_nt(DD[:, 0:384], wq).astype(BF16)

    li = pltpu.make_async_copy(IG.at[mine, :], ig_out.at[:, col_c], loc_sem.at[3])
    li.start()
    si = rcopy(IG.at[theirs, :], ig_out.at[:, col_c], sib_s.at[4], sib_r.at[4], sib)
    si.start()

    @pl.loop(0, 8)
    def _(i):
        rb = at_turn(i)
        opp_copy(rb, 0).wait_recv()
        at = rows(kn * CHUNK + rb * BLOCK, BLOCK, 32)
        got = Ropp[rows(rb * BLOCK, BLOCK, 32), :]
        PX[at, lane(half_f)] = (PX[at, lane(half_f)].astype(F32) + got.astype(F32)).astype(BF16)
        nb_copy(rb, half_f).start()

    y_ring[0](1)
    y_ring[1](1)
    z_ring[0](1)
    z_ring[1](1)
    y_ring[0](0)
    z_ring[0](0)

    def x_done(zr):
        at = rows(zr * BLOCK, BLOCK, 32)

        @when(is_opp)
        def _():
            own_copy(zr).wait_recv()

        for src in (0, 1):
            for h in (0, 1):
                r = Rn.at[src, at, pl.ds(128 * h, 128)]
                rcopy(r, r, nb_s.at[0, 0], nb_r.at[src, zr, h], sib).wait_recv()
        total = Ro[at, :].astype(F32) + Rn[0, at, :].astype(F32) + Rn[1, at, :].astype(F32)
        Sb[at, :] = total.astype(BF16)
        for s in (0, 1):
            i = zr * 2 + s

            @when(i != z)
            def _():
                dz_copy(i).start()

            @when(i != y)
            def _():
                dy_copy(i).start()

    x_done(0)
    x_done(1)
    SY[...] = y_ring[2]().astype(BF16)
    dx_send(SY, DxY, dxy_s, dxy_r)
    SZ[...] = z_ring[2]().astype(BF16)
    dx_send(SZ, DxZ, dxz_s, dxz_r)
    x_done(2)
    x_done(3)

    Dz[z] = Sb[rows(z * UNITS, UNITS, 16), 0:128]
    Dy[y] = Sb[rows(y * UNITS, UNITS, 16), 128:256]
    Ty[0:UNITS, 128:256] = dx_receive(DxZ, dxz_s, dxz_r)
    Tz[0:UNITS, 128:256] = dx_receive(DxY, dxy_s, dxy_r)

    @pl.loop(0, 8)
    def _(k):
        @when(k != z)
        def _():
            rcopy(Dz.at[k], Dz.at[k], dz_s.at[k], dz_r.at[k], dev(x, y, k, c)).wait_recv()

        Ty[0:UNITS, 0:128] = Ty[0:UNITS, 0:128] + Dz[k].astype(F32)

    for k in range(8):
        unit = Ty[10 * k : 10 * k + 16, :].astype(BF16)
        Uy[k] = unit
        to_self = feeds_self & (self_k == k)

        @when(to_self)
        def _():
            Fy[y] = unit

        @unless(to_self)
        def _():
            fy_copy(k).start()

    @pl.loop(0, 8)
    def _(k):
        @when(k != y)
        def _():
            rcopy(Dy.at[k], Dy.at[k], dy_s.at[k], dy_r.at[k], dev(x, k, z, c)).wait_recv()

        Tz[0:UNITS, 0:128] = Tz[0:UNITS, 0:128] + Dy[k].astype(F32)

    for k in range(8):
        unit = Tz[10 * k : 10 * k + 16, :].astype(BF16)
        Uz[k] = unit

        @when(k == z)
        def _():
            Fz[z] = unit

        @when(k != z)
        def _():
            fz_copy(k).start()

    total = None
    for k in range(8):
        @unless(feeds_self & (y == k))
        def _():
            rcopy(Fy.at[k], Fy.at[k], fy_s.at[k], fy_r.at[k], sib).wait_recv()

        total = Fy[k].astype(F32) if total is None else total + Fy[k].astype(F32)
    total = total * (1.0 / 512.0)
    wg_out[:, 0, :] = total[0:10, 0:128]
    wg_out[:, 3, :] = total[0:10, 128:256]
    total = None
    for k in range(8):
        @when(z != k)
        def _():
            rcopy(Fz.at[k], Fz.at[k], fz_s.at[k], fz_r.at[k], sib).wait_recv()

        total = Fz[k].astype(F32) if total is None else total + Fz[k].astype(F32)
    total = total * (1.0 / 512.0)
    wg_out[:, 1, :] = total[0:10, 0:128]
    wg_out[:, 2, :] = total[0:10, 128:256]

    sh.wait_send()
    so.wait_send()

    @when(active)
    def _():
        g1_copy(0, zl).wait_send()
        g1_copy(1, zl).wait_send()
        for dy in range(1, 8):
            cp_copy(dy).wait_send()
        for sub, d in order:
            b_copy(y, 0, d, sub).wait_send()

    for sub, d in order:
        c_copy(z, 0, d, sub).wait_send()
    for t in range(1, 4):
        for d in (0, 1):
            s = ((y + 8 - t) % 8, (y + t) % 8)[d]
            zs = ((z + 8 - t) % 8, (z + t) % 8)[d]
            for sub in (0, 1):
                if t < 3 or sub == d:
                    c_copy(zs, t, d, sub).wait_send()

                    @when(s // 4 == c)
                    def _():
                        b_copy(s, t, d, sub).wait_send()

    sa.wait_send()
    sd.wait_send()

    li.wait()
    si.wait()
    y_ring[3]()
    z_ring[3]()
    dx_wait(SY, DxY, dxy_s, dxy_r)
    dx_wait(SZ, DxZ, dxz_s, dxz_r)

    @pl.loop(0, 8)
    def _(k):
        nb_copy(k, half_f).wait_send()
        nb_copy(k, half_d).wait_send()

        @when(is_opp)
        def _():
            opp_copy(k, 0).wait_send()
            opp_copy(k, 1).wait_send()

        @when(k != z)
        def _():
            dz_copy(k).wait_send()

        @when(k != y)
        def _():
            dy_copy(k).wait_send()

    @unless(is_opp)
    def _():
        @pl.loop(0, 4)
        def _(zr):
            own_copy(zr).wait_send()

    @pl.loop(0, 8)
    def _(k):
        @when(k != z)
        def _():
            fz_copy(k).wait_send()

        @unless(feeds_self & (self_k == k))
        def _():
            fy_copy(k).wait_send()


def hand_over(ig, wg, ig_out, wg_out, held, held_wg, into, out):
    def moves(source, target, sem):
        pairs = [(source[1], target[1], 8)]
        for k in range(8):
            at = pl.ds(16 * k, 16)
            pairs.append((source[0].at[at, :], target[0].at[at, :], k))
        return [pltpu.make_async_copy(a, b, sem.at[k]) for a, b, k in pairs]

    inward = moves((ig, wg), (held, held_wg), into)
    outward = moves((held, held_wg), (ig_out, wg_out), out)
    for move in inward:
        move.start()
    for first, second in zip(inward, outward):
        first.wait()
        second.start()
    for move in outward:
        move.wait()


def local(hidden, out_grad, weights):
    table = jnp.asarray(rope_tables())
    turn = jnp.asarray(turn_table(), BF16)
    vmem = pl.BlockSpec(memory_space=pltpu.VMEM)
    hbm = pl.BlockSpec(memory_space=pltpu.HBM)
    dma = pltpu.SemaphoreType.DMA
    v = pltpu.VMEM
    results = (
        jax.ShapeDtypeStruct(hidden.shape, BF16),
        jax.ShapeDtypeStruct((10, 4, HD), F32),
    )
    found = pl.pallas_call(
        kernel,
        out_shape=results,
        in_specs=[hbm] * 5,
        out_specs=(hbm, vmem),
        scratch_shapes=[
            v((256, HALF), BF16),
            v((256, HALF), BF16),
            v((4, 4, ITEM, HD), BF16),
            v((HALF, 256), BF16),
            v((HALF, 256), BF16),
            v((HALF, 256), BF16),
            v((2, SEQ, HD), F32),
            v((ITEM, ITEM), BF16),
            v((256, 512), F32),
            v((SEQ, 512), F32),
            v((256, 512), BF16),
            v((HALF, 256), BF16),
            v((CHUNK, 128), BF16),
            v((2, 640, 256), BF16),
            v((640, 256), BF16),
            v((640, 256), BF16),
            v((8, 320, 128), BF16),
            v((8, 320, 128), BF16),
            v((2, 4, 320, 128), BF16),
            v((2, 4, 320, 128), BF16),
            v((8, UNITS, 128), BF16),
            v((8, UNITS, 128), BF16),
            v((4, UNITS, 128), BF16),
            v((4, UNITS, 128), BF16),
            v((320, 128), BF16),
            v((320, 128), BF16),
            v((96, 256), F32),
            v((96, 256), F32),
            v((8, 16, 256), BF16),
            v((8, 16, 256), BF16),
            v((8, 16, 256), BF16),
            v((8, 16, 256), BF16),
            v((256, HALF), BF16),
            dma((7,)), dma((5,)), dma((5,)),
            dma((2,)), dma((2,)),
            dma((4, 2, 2)), dma((4, 2)),
            dma((8,)), dma((4,)),
            dma((4, 2, 2)), dma((8, 2)),
            dma((8, 2)), dma((8,)),
            dma((8, 2)), dma((2, 4, 2)),
            dma((4,)), dma((4,)),
            dma((4, 2)), dma((4, 2)),
            dma((4, 2)), dma((4, 2)),
            dma((8,)), dma((8,)),
            dma((8,)), dma((8,)),
            dma((4,)), dma((4,)),
            dma((4,)), dma((4,)),
            dma((8,)), dma((8,)),
            dma((8,)), dma((8,)),
        ],
        compiler_params=pltpu.CompilerParams(
            collective_id=0, has_side_effects=True, vmem_limit_bytes=62 * 1024 * 1024
        ),
    )(hidden, out_grad, weights, table, turn)
    input_grad, weight_grads = pl.pallas_call(
        hand_over,
        out_shape=results,
        in_specs=[hbm, hbm],
        out_specs=(hbm, hbm),
        scratch_shapes=[v((SEQ, 2 * HALF), BF16), v((10, 4, HD), F32), dma((9,)), dma((9,))],
    )(*found)
    return input_grad, jnp.transpose(weight_grads, (1, 0, 2))


def solution(mesh):
    placed = (P(("cuts", "chip"), None), P(("cuts", "chip"), None), P(None, "chip", None))
    return jax.shard_map(
        local,
        mesh=mesh,
        in_specs=placed,
        out_specs=(P(("cuts", "chip"), None), P(None, ("cuts", "chip"), None)),
        check_vma=False,
    )
```

```python
import jax
import jax.numpy as jnp
import numpy as np
from jax import lax
from jax.experimental import pallas as pl
from jax.experimental.pallas import tpu as pltpu
from jax.sharding import PartitionSpec as P

MESH = pl.DeviceIdType.MESH
F32 = jnp.float32
BF16 = jnp.bfloat16

HD = 128
SEQ = 128
HALF = 2560
ITEM = 640
CHUNK = 1280
BLOCK = 160
UNITS = 80


def rope_tables():
    half = HD // 2
    rates = 10000.0 ** (-(np.arange(half) * 2.0) / HD)
    angle = np.arange(SEQ)[:, None] * rates[None, :]
    cosine, sine = np.cos(angle), np.sin(angle)
    return np.stack(
        [np.concatenate([cosine, cosine], axis=1), np.concatenate([-sine, sine], axis=1)]
    ).astype(np.float32)


def turn_table():
    order = np.arange(ITEM).reshape(2, 2, 8, 20).transpose(1, 2, 0, 3).reshape(-1)
    table = np.zeros((ITEM, ITEM), np.float32)
    table[np.arange(ITEM), order] = 1.0
    return table


def dot(a, b):
    return jnp.dot(a, b, preferred_element_type=F32)


def dot_nt(a, b):
    return lax.dot_general(a, b, (((1,), (1,)), ((), ())), preferred_element_type=F32)


def kernel(
    hid, og, wts, cs, turn, ig_out, wg_out,
    Hb, Ob, W, HT, HP, OT, CS, TN, acc, accr, DD,
    PX, Ropp, Rn, Ro, Sb, PY, PZ, RY, RZ, Dz, Dy, DxY, DxZ, SY, SZ, Ty, Tz, Uy, Uz, Fy, Fz, IG,
    loc_sem, sib_s, sib_r, g1_s, g1_r, b_s, b_r, cp_s, cp_r, c_s, c_r,
    opp_s, opp_r, nb_s, nb_r, own_s, own_r, ry_s, ry_r, rz_s, rz_r,
    dz_s, dz_r, dy_s, dy_r, dxy_s, dxy_r, dxz_s, dxz_r, fy_s, fy_r, fz_s, fz_r,
):
    ci = lax.axis_index("cuts")
    ch = lax.axis_index("chip")
    x = ci // 8
    zh = (ci // 2) % 4
    c = ci % 2
    y = ch // 2
    zl = ch % 2
    z = zh * 2 + zl
    o = 1 - c

    def dev(x_, y_, z_, c_):
        return (x_ * 8 + (z_ // 2) * 2 + c_, y_ * 2 + z_ % 2)

    def rcopy(src, dst, ss, rs, to):
        return pltpu.make_async_remote_copy(
            src_ref=src, dst_ref=dst, send_sem=ss, recv_sem=rs, device_id=to, device_id_type=MESH
        )

    def when(cond):
        return pl.when(cond)

    def unless(cond):
        return pl.when(jnp.logical_not(cond))

    def rows(start, size, step):
        return pl.ds(pl.multiple_of(start, step), size)

    sib = dev(x, y, z, o)
    yq = y % 4
    active = y // 4 == c
    mine = rows(c * SEQ, SEQ, SEQ)
    theirs = rows(o * SEQ, SEQ, SEQ)
    col_c = rows(c * HALF, HALF, HALF)
    col_o = rows(o * HALF, HALF, HALF)
    yp, ym = (y + 1) % 8, (y + 7) % 8
    zp, zm = (z + 1) % 8, (z + 7) % 8
    xp, xm = (x + 1) % 4, (x + 3) % 4

    lh = pltpu.make_async_copy(hid.at[:, col_c], Hb.at[mine, :], loc_sem.at[0])
    lo = pltpu.make_async_copy(og.at[:, col_c], Ob.at[mine, :], loc_sem.at[1])
    lw = pltpu.make_async_copy(
        wts.at[pl.ds(0, 2)], W.at[pl.ds(0, 2), yq, rows(zl * 320, 320, 64), :], loc_sem.at[2]
    )
    lq = pltpu.make_async_copy(
        wts.at[pl.ds(2, 2), rows(zh * UNITS, UNITS, 16), :],
        W.at[pl.ds(2, 2), yq, rows(zl * 320 + zh * UNITS, UNITS, 16), :],
        loc_sem.at[6],
    )
    lc = pltpu.make_async_copy(cs, CS, loc_sem.at[4])
    lt = pltpu.make_async_copy(turn, TN, loc_sem.at[5])

    @when(active)
    def _():
        lw.start()
        lq.start()

    lh.start()
    lo.start()
    lt.start()
    lc.start()

    bar = pltpu.get_barrier_semaphore()

    def greet(to):
        pl.semaphore_signal(bar, inc=1, device_id=to, device_id_type=MESH)

    for dy in range(1, 8):
        for l in (0, 1):
            greet(dev(x, (y + dy) % 8, zh * 2 + l, c))
    for dz in range(1, 8):
        greet(dev(x, y, (z + dz) % 8, c))
    for dx in (1, 2, 3):
        for cc in (0, 1):
            greet(dev((x + dx) % 4, y, z, cc))
    greet(sib)
    acc[...] = jnp.zeros_like(acc)
    Ty[...] = jnp.zeros_like(Ty)
    Tz[...] = jnp.zeros_like(Tz)
    pl.semaphore_wait(bar, 14 + 7 + 6 + 1)

    def cp_copy(dy):
        at = rows(zh * UNITS, UNITS, 16)
        return rcopy(
            wts.at[pl.ds(2, 2), at, :],
            W.at[pl.ds(2, 2), yq, rows(zl * 320 + zh * UNITS, UNITS, 16), :],
            cp_s.at[dy], cp_r.at[yq], dev(x, (y + dy) % 8, z, c),
        )

    def g1_copy(i, l):
        return rcopy(
            wts.at[pl.ds(0, 2), pl.ds(160 * i, 160), :],
            W.at[pl.ds(0, 2), yq, rows(l * 320 + 160 * i, 160, 32), :],
            g1_s.at[i], g1_r.at[i], dev(x, y, (zp, zm)[i], c),
        )

    @when(active)
    def _():
        for dy in (1, 7, 2, 6, 3, 5, 4):
            cp_copy(dy).start()
        g1_copy(0, zl).start()
        g1_copy(1, zl).start()

    sh = rcopy(hid.at[:, col_o], Hb.at[mine, :], sib_s.at[0], sib_r.at[0], sib)
    so = rcopy(og.at[:, col_o], Ob.at[mine, :], sib_s.at[1], sib_r.at[1], sib)
    sh.start()
    so.start()

    def b_copy(s, t, d, sub):
        r = W.at[sub, s % 4]
        return rcopy(r, r, b_s.at[t, d, sub], b_r.at[s % 4, sub], dev(x, (yp, ym)[d], z, c))

    def c_copy(s, t, d, sub):
        r = W.at[2 + sub, :, rows((s % 2) * 320 + (s // 2) * UNITS, UNITS, 16), :]
        return rcopy(r, r, c_s.at[t, d, sub], c_r.at[s, sub], dev(x, y, (zp, zm)[d], c))

    def project_qk(s):
        at = rows((s % 4) * ITEM, ITEM, 128)
        acc[:, 0:256] += dot(Hb[:, at], jnp.concatenate([W[0, s % 4], W[1, s % 4]], axis=1))

    def transpose(src, dst, q):
        turned = src[:, q * ITEM : (q + 1) * ITEM].T
        for i in range(4):
            zr, cr = (q % 2) * 2 + i // 2, i % 2
            at = (q // 2) * CHUNK + (cr * 4 + zr) * BLOCK
            dst[at : at + BLOCK, :] = turned[i * BLOCK : (i + 1) * BLOCK, :]

    def transpose_turned(xr):
        low = dot_nt(TN[...], Hb[:, xr * CHUNK : xr * CHUNK + ITEM])
        high = dot_nt(TN[...], Hb[:, xr * CHUNK + ITEM : (xr + 1) * CHUNK])
        for g in range(16):
            at = xr * CHUNK + g * UNITS
            both = jnp.concatenate([low[g * 40 : g * 40 + 40], high[g * 40 : g * 40 + 40]], axis=0)
            HP[at : at + UNITS, :] = both.astype(BF16)

    order = ((0, 0), (1, 1), (1, 0), (0, 1))

    @when(active)
    def _():
        lw.wait()
        lq.wait()
        g1_copy(0, 1 - zl).wait_recv()
        g1_copy(1, 1 - zl).wait_recv()
        for sub, d in order:
            b_copy(y, 0, d, sub).start()

    for k in range(4):
        @unless(active & (k == yq))
        def _():
            at = rows(zl * 320 + zh * UNITS, UNITS, 16)
            r = W.at[pl.ds(2, 2), k, at, :]
            rcopy(r, r, cp_s.at[1], cp_r.at[k], dev(x, yp, z, c)).wait_recv()

    for sub, d in order:
        c_copy(z, 0, d, sub).start()

    lh.wait()
    sh.wait_recv()
    for q in range(4):
        transpose(Hb, HT, q)

    @when(active)
    def _():
        project_qk(y)

    for t in range(1, 5):
        ys = ((y + 8 - t) % 8, (y + t) % 8)
        zs = ((z + 8 - t) % 8, (z + t) % 8)
        if t < 4:
            for i in (0, 1):
                for d in (0, 1):
                    s = ys[d]
                    sub = i if d == 0 else 1 - i

                    @when(s // 4 == c)
                    def _():
                        b_copy(s, 0, 0, sub).wait_recv()
                        if t < 3 or sub == d:
                            b_copy(s, t, d, sub).start()

                for d in (0, 1):
                    s = zs[d]
                    sub = i if d == 0 else 1 - i
                    c_copy(s, 0, 0, sub).wait_recv()
                    if t < 3 or sub == d:
                        c_copy(s, t, d, sub).start()

            if t == 1:
                lt.wait()
                transpose_turned(0)
                transpose_turned(1)
            if t == 2:
                lo.wait()
                so.wait_recv()
                for q in range(4):
                    transpose(Ob, OT, q)
            for d in (0, 1):
                s = ys[d]

                @when(s // 4 == c)
                def _():
                    project_qk(s)

        else:
            s = ys[0]

            @when(s // 4 == c)
            def _():
                b_copy(s, 0, 0, 0).wait_recv()
                b_copy(s, 0, 0, 1).wait_recv()
                project_qk(s)

            c_copy(zs[0], 0, 0, 0).wait_recv()
            c_copy(zs[0], 0, 0, 1).wait_recv()

    wv = jnp.concatenate([W[2, k] for k in range(4)], axis=0)
    acc[:, 256:384] = dot(Hb[...], wv)
    wo = jnp.concatenate([W[3, k] for k in range(4)], axis=0)
    acc[:, 384:512] = dot(Ob[...], wo)

    sa = rcopy(acc.at[theirs, :], accr, sib_s.at[2], sib_r.at[2], sib)
    sa.start()
    lc.wait()
    cosine, sine = CS[0], CS[1]

    def rope(v, sgn):
        return v * cosine + pltpu.roll(v, 64, 1) * (sine * sgn)

    scale = 1.0 / np.sqrt(np.float32(HD))
    at_row = lax.broadcasted_iota(jnp.int32, (SEQ, SEQ), 0)
    at_col = lax.broadcasted_iota(jnp.int32, (SEQ, SEQ), 1)
    sa.wait_recv()
    summed = acc[mine, :] + accr[...]
    query = rope(summed[:, 0:128], 1.0).astype(BF16)
    keys = rope(summed[:, 128:256], 1.0).astype(BF16)
    values = summed[:, 256:384].astype(BF16)
    d_attn = summed[:, 384:512].astype(BF16)
    scores = dot_nt(query, keys) * scale
    d_prob = dot_nt(d_attn, values)
    scores = jnp.where(at_col <= at_row, scores, -jnp.inf)
    expo = jnp.exp(scores - jnp.max(scores, axis=1, keepdims=True))
    prob = expo / jnp.sum(expo, axis=1, keepdims=True)
    prob_b = prob.astype(BF16)
    attn = dot(prob_b, values)
    d_score = prob * (d_prob - jnp.sum(prob * d_prob, axis=1, keepdims=True)) * scale
    d_query = rope(dot(d_score.astype(BF16), keys), -1.0)
    d_key = rope(dot(d_score.T.astype(BF16), query), -1.0)
    d_value = dot(prob.T.astype(BF16), d_attn)
    DD[mine, :] = jnp.concatenate([d_query, d_key, d_value, attn], axis=1).astype(BF16)
    sd = rcopy(DD.at[mine, :], DD.at[mine, :], sib_s.at[3], sib_r.at[3], sib)
    sd.start()
    rcopy(DD.at[theirs, :], DD.at[theirs, :], sib_s.at[3], sib_r.at[3], sib).wait_recv()

    dd = (2 * c + 4 - x) % 4
    is_opp = (dd == 1) | (dd == 2)
    plus = dd < 2
    kn = jnp.where((dd == 0) | (dd == 2), 1, 0)
    ks = 1 - kn
    xn = jnp.where(plus, xp, xm)
    slot = jnp.where(plus, 0, 1)
    half_f = jnp.where(plus, 0, 1)
    half_d = 1 - half_f

    def lane(h):
        return pl.ds(pl.multiple_of(h * 128, 128), 128)

    def x_piece(k, rb):
        at = rows(k * CHUNK + rb * BLOCK, BLOCK, 32)
        left = dot(HT[at, :], DD[:, 0:128])
        right = dot(HP[at, :], DD[:, 128:256])
        return jnp.concatenate([left, right], axis=1).astype(BF16)

    def opp_copy(rb, h):
        return rcopy(
            PX.at[rows(ks * CHUNK + rb * BLOCK, BLOCK, 32), lane(h)],
            Ropp.at[rows(rb * BLOCK, BLOCK, 32), :],
            opp_s.at[rb, h], opp_r.at[rb], dev((xp, xm)[h], y, z, c),
        )

    def nb_copy(rb, h):
        cr, zr = rb // 4, rb % 4
        return rcopy(
            PX.at[rows(kn * CHUNK + rb * BLOCK, BLOCK, 32), lane(h)],
            Rn.at[slot, rows(zr * BLOCK, BLOCK, 32), lane(h)],
            nb_s.at[rb, h], nb_r.at[slot, zr, h], dev(xn, y, z, cr),
        )

    def own_copy(zr):
        return rcopy(
            PX.at[rows(ks * CHUNK + (o * 4 + zr) * BLOCK, BLOCK, 32), :],
            Ro.at[rows(zr * BLOCK, BLOCK, 32), :],
            own_s.at[zr], own_r.at[zr], sib,
        )

    def ring(pos, mat, lanes, PR, RR, s_sem, r_sem, to):
        def chunk_of(k, d):
            return (pos + (k if d == 0 else 8 - k)) % 8

        def compute(i):
            lhs = jnp.concatenate(
                [mat[rows(g * 640 + i * UNITS, UNITS, 16), :] for g in range(4)], axis=0
            )
            PR[i] = dot(lhs, DD[:, lanes : lanes + 128]).astype(BF16)

        def copy(k, d):
            i = chunk_of(k, d)
            at = pl.ds(160 * d, 160) if k == 4 else pl.ds(0, 320)
            return rcopy(
                PR.at[i, at, :], RR.at[d, k - 1, at, :], s_sem.at[k - 1, d], r_sem.at[k - 1, d], to[d]
            )

        def step(k):
            for d in (0, 1):
                i = chunk_of(k, d)
                if k == 3:
                    copy(4, d).wait_recv()
                    at = slice(160 * d, 160 * d + 160)
                    PR[i, at, :] = (PR[i, at, :].astype(F32) + RR[d, 3, at, :].astype(F32)).astype(BF16)
                elif k < 3:
                    copy(k + 1, d).wait_recv()
                    PR[i] = (PR[i].astype(F32) + RR[d, k].astype(F32)).astype(BF16)
                copy(k, d).start()

        def finish():
            copy(1, 0).wait_recv()
            copy(1, 1).wait_recv()
            return PR[pos].astype(F32) + RR[0, 0].astype(F32) + RR[1, 0].astype(F32)

        def wait_sends():
            for k in range(1, 5):
                for d in (0, 1):
                    copy(k, d).wait_send()

        def compute_for(k):
            compute(chunk_of(k, 0))
            if k not in (0, 4):
                compute(chunk_of(k, 1))

        return compute_for, step, finish, wait_sends

    y_ring = ring(y, HP, 256, PY, RY, ry_s, ry_r, (dev(x, yp, z, c), dev(x, ym, z, c)))
    z_ring = ring(z, OT, 384, PZ, RZ, rz_s, rz_r, (dev(x, y, zp, c), dev(x, y, zm, c)))

    def dx_copy(S, R, a, cr, s_sem, r_sem):
        return rcopy(
            S.at[pl.ds((a * 2 + cr) * UNITS, UNITS), :], R.at[x],
            s_sem.at[a * 2 + cr], r_sem.at[x], dev(2 * c + a, y, z, cr),
        )

    def dx_send(S, R, s_sem, r_sem):
        for a in (0, 1):
            for cr in (0, 1):
                to_self = (2 * c + a == x) & (cr == c)

                @when(to_self)
                def _():
                    R[x] = S[(a * 2 + cr) * UNITS : (a * 2 + cr + 1) * UNITS, :]

                @unless(to_self)
                def _():
                    dx_copy(S, R, a, cr, s_sem, r_sem).start()

    def dx_receive(R, s_sem, r_sem):
        total = None
        for k in range(4):
            @unless((k == x) & (x // 2 == c))
            def _():
                rcopy(R.at[k], R.at[k], s_sem.at[0], r_sem.at[k], sib).wait_recv()

            total = R[k].astype(F32) if total is None else total + R[k].astype(F32)
        return total

    def dx_wait(S, R, s_sem, r_sem):
        for a in (0, 1):
            for cr in (0, 1):
                @unless((2 * c + a == x) & (cr == c))
                def _():
                    dx_copy(S, R, a, cr, s_sem, r_sem).wait_send()

    def dz_copy(i):
        return rcopy(
            Sb.at[rows(i * UNITS, UNITS, 16), pl.ds(0, 128)], Dz.at[z],
            dz_s.at[i], dz_r.at[z], dev(x, y, i, c),
        )

    def dy_copy(i):
        return rcopy(
            Sb.at[rows(i * UNITS, UNITS, 16), pl.ds(128, 128)], Dy.at[y],
            dy_s.at[i], dy_r.at[y], dev(x, i, z, c),
        )

    def fy_copy(k):
        yr, lr = zl * 4 + k // 2, k % 2
        return rcopy(Uy.at[k], Fy.at[y], fy_s.at[k], fy_r.at[y], dev(x, yr, zh * 2 + lr, c))

    def fz_copy(k):
        return rcopy(Uz.at[k], Fz.at[z], fz_s.at[k], fz_r.at[z], dev(x, y, k, c))

    self_k = yq * 2 + zl
    feeds_self = zl == y // 4

    def at_turn(i):
        return (i % 2) * 4 + i // 2

    def neighbour_pieces():
        @pl.loop(0, 8)
        def _(i):
            rb = at_turn(i)
            PX[rows(kn * CHUNK + rb * BLOCK, BLOCK, 32), :] = x_piece(kn, rb)
            nb_copy(rb, half_d).start()

    y_ring[0](4)
    y_ring[1](4)
    z_ring[0](4)
    z_ring[1](4)

    @when(is_opp)
    def _():
        @pl.loop(0, 8)
        def _(i):
            rb = at_turn(i)
            PX[rows(ks * CHUNK + rb * BLOCK, BLOCK, 32), :] = x_piece(ks, rb)
            opp_copy(rb, 0).start()
            opp_copy(rb, 1).start()

    @unless(is_opp)
    def _():
        neighbour_pieces()

    y_ring[0](3)
    y_ring[1](3)
    z_ring[0](3)
    z_ring[1](3)

    @when(is_opp)
    def _():
        neighbour_pieces()

    @unless(is_opp)
    def _():
        @pl.loop(0, 4)
        def _(zr):
            PX[rows(ks * CHUNK + (o * 4 + zr) * BLOCK, BLOCK, 32), :] = x_piece(ks, o * 4 + zr)
            own_copy(zr).start()

        @pl.loop(0, 4)
        def _(zr):
            Ro[rows(zr * BLOCK, BLOCK, 32), :] = x_piece(ks, c * 4 + zr)

    y_ring[0](2)
    y_ring[1](2)
    z_ring[0](2)
    z_ring[1](2)

    @pl.loop(0, 4)
    def _(q):
        wq = jnp.concatenate([W[0, q], W[1, q], W[2, q]], axis=1)
        IG[:, rows(q * ITEM, ITEM, 128)] = dot_nt(DD[:, 0:384], wq).astype(BF16)

    li = pltpu.make_async_copy(IG.at[mine, :], ig_out.at[:, col_c], loc_sem.at[3])
    li.start()
    si = rcopy(IG.at[theirs, :], ig_out.at[:, col_c], sib_s.at[4], sib_r.at[4], sib)
    si.start()

    @pl.loop(0, 8)
    def _(i):
        rb = at_turn(i)
        opp_copy(rb, 0).wait_recv()
        at = rows(kn * CHUNK + rb * BLOCK, BLOCK, 32)
        got = Ropp[rows(rb * BLOCK, BLOCK, 32), :]
        PX[at, lane(half_f)] = (PX[at, lane(half_f)].astype(F32) + got.astype(F32)).astype(BF16)
        nb_copy(rb, half_f).start()

    y_ring[0](1)
    y_ring[1](1)
    z_ring[0](1)
    z_ring[1](1)
    y_ring[0](0)
    z_ring[0](0)

    def x_done(zr):
        at = rows(zr * BLOCK, BLOCK, 32)

        @when(is_opp)
        def _():
            own_copy(zr).wait_recv()

        for src in (0, 1):
            for h in (0, 1):
                r = Rn.at[src, at, pl.ds(128 * h, 128)]
                rcopy(r, r, nb_s.at[0, 0], nb_r.at[src, zr, h], sib).wait_recv()
        total = Ro[at, :].astype(F32) + Rn[0, at, :].astype(F32) + Rn[1, at, :].astype(F32)
        Sb[at, :] = total.astype(BF16)
        for s in (0, 1):
            i = zr * 2 + s

            @when(i != z)
            def _():
                dz_copy(i).start()

            @when(i != y)
            def _():
                dy_copy(i).start()

    x_done(0)
    x_done(1)
    SY[...] = y_ring[2]().astype(BF16)
    dx_send(SY, DxY, dxy_s, dxy_r)
    SZ[...] = z_ring[2]().astype(BF16)
    dx_send(SZ, DxZ, dxz_s, dxz_r)
    x_done(2)
    x_done(3)

    Dz[z] = Sb[rows(z * UNITS, UNITS, 16), 0:128]
    Dy[y] = Sb[rows(y * UNITS, UNITS, 16), 128:256]
    Ty[0:UNITS, 128:256] = dx_receive(DxZ, dxz_s, dxz_r)
    Tz[0:UNITS, 128:256] = dx_receive(DxY, dxy_s, dxy_r)

    @pl.loop(0, 8)
    def _(k):
        @when(k != z)
        def _():
            rcopy(Dz.at[k], Dz.at[k], dz_s.at[k], dz_r.at[k], dev(x, y, k, c)).wait_recv()

        Ty[0:UNITS, 0:128] = Ty[0:UNITS, 0:128] + Dz[k].astype(F32)

    for k in range(8):
        unit = Ty[10 * k : 10 * k + 16, :].astype(BF16)
        Uy[k] = unit
        to_self = feeds_self & (self_k == k)

        @when(to_self)
        def _():
            Fy[y] = unit

        @unless(to_self)
        def _():
            fy_copy(k).start()

    @pl.loop(0, 8)
    def _(k):
        @when(k != y)
        def _():
            rcopy(Dy.at[k], Dy.at[k], dy_s.at[k], dy_r.at[k], dev(x, k, z, c)).wait_recv()

        Tz[0:UNITS, 0:128] = Tz[0:UNITS, 0:128] + Dy[k].astype(F32)

    for k in range(8):
        unit = Tz[10 * k : 10 * k + 16, :].astype(BF16)
        Uz[k] = unit

        @when(k == z)
        def _():
            Fz[z] = unit

        @when(k != z)
        def _():
            fz_copy(k).start()

    total = None
    for k in range(8):
        @unless(feeds_self & (y == k))
        def _():
            rcopy(Fy.at[k], Fy.at[k], fy_s.at[k], fy_r.at[k], sib).wait_recv()

        total = Fy[k].astype(F32) if total is None else total + Fy[k].astype(F32)
    total = total * (1.0 / 512.0)
    wg_out[:, 0, :] = total[0:10, 0:128]
    wg_out[:, 3, :] = total[0:10, 128:256]
    total = None
    for k in range(8):
        @when(z != k)
        def _():
            rcopy(Fz.at[k], Fz.at[k], fz_s.at[k], fz_r.at[k], sib).wait_recv()

        total = Fz[k].astype(F32) if total is None else total + Fz[k].astype(F32)
    total = total * (1.0 / 512.0)
    wg_out[:, 1, :] = total[0:10, 0:128]
    wg_out[:, 2, :] = total[0:10, 128:256]

    sh.wait_send()
    so.wait_send()

    @when(active)
    def _():
        g1_copy(0, zl).wait_send()
        g1_copy(1, zl).wait_send()
        for dy in range(1, 8):
            cp_copy(dy).wait_send()
        for sub, d in order:
            b_copy(y, 0, d, sub).wait_send()

    for sub, d in order:
        c_copy(z, 0, d, sub).wait_send()
    for t in range(1, 4):
        for d in (0, 1):
            s = ((y + 8 - t) % 8, (y + t) % 8)[d]
            zs = ((z + 8 - t) % 8, (z + t) % 8)[d]
            for sub in (0, 1):
                if t < 3 or sub == d:
                    c_copy(zs, t, d, sub).wait_send()

                    @when(s // 4 == c)
                    def _():
                        b_copy(s, t, d, sub).wait_send()

    sa.wait_send()
    sd.wait_send()

    li.wait()
    si.wait()
    y_ring[3]()
    z_ring[3]()
    dx_wait(SY, DxY, dxy_s, dxy_r)
    dx_wait(SZ, DxZ, dxz_s, dxz_r)

    @pl.loop(0, 8)
    def _(k):
        nb_copy(k, half_f).wait_send()
        nb_copy(k, half_d).wait_send()

        @when(is_opp)
        def _():
            opp_copy(k, 0).wait_send()
            opp_copy(k, 1).wait_send()

        @when(k != z)
        def _():
            dz_copy(k).wait_send()

        @when(k != y)
        def _():
            dy_copy(k).wait_send()

    @unless(is_opp)
    def _():
        @pl.loop(0, 4)
        def _(zr):
            own_copy(zr).wait_send()

    @pl.loop(0, 8)
    def _(k):
        @when(k != z)
        def _():
            fz_copy(k).wait_send()

        @unless(feeds_self & (self_k == k))
        def _():
            fy_copy(k).wait_send()


def hand_over(ig, wg, ig_out, wg_out, held, held_wg, into, out):
    def moves(source, target, sem):
        pairs = [(source[1], target[1], 8)]
        for k in range(8):
            at = pl.ds(16 * k, 16)
            pairs.append((source[0].at[at, :], target[0].at[at, :], k))
        return [pltpu.make_async_copy(a, b, sem.at[k]) for a, b, k in pairs]

    inward = moves((ig, wg), (held, held_wg), into)
    outward = moves((held, held_wg), (ig_out, wg_out), out)
    for move in inward:
        move.start()
    for first, second in zip(inward, outward):
        first.wait()
        second.start()
    for move in outward:
        move.wait()


def local(hidden, out_grad, weights):
    table = jnp.asarray(rope_tables())
    turn = jnp.asarray(turn_table(), BF16)
    vmem = pl.BlockSpec(memory_space=pltpu.VMEM)
    hbm = pl.BlockSpec(memory_space=pltpu.HBM)
    dma = pltpu.SemaphoreType.DMA
    v = pltpu.VMEM
    results = (
        jax.ShapeDtypeStruct(hidden.shape, BF16),
        jax.ShapeDtypeStruct((10, 4, HD), F32),
    )
    found = pl.pallas_call(
        kernel,
        out_shape=results,
        in_specs=[hbm] * 5,
        out_specs=(hbm, vmem),
        scratch_shapes=[
            v((256, HALF), BF16),
            v((256, HALF), BF16),
            v((4, 4, ITEM, HD), BF16),
            v((HALF, 256), BF16),
            v((HALF, 256), BF16),
            v((HALF, 256), BF16),
            v((2, SEQ, HD), F32),
            v((ITEM, ITEM), BF16),
            v((256, 512), F32),
            v((SEQ, 512), F32),
            v((256, 512), BF16),
            v((HALF, 256), BF16),
            v((CHUNK, 128), BF16),
            v((2, 640, 256), BF16),
            v((640, 256), BF16),
            v((640, 256), BF16),
            v((8, 320, 128), BF16),
            v((8, 320, 128), BF16),
            v((2, 4, 320, 128), BF16),
            v((2, 4, 320, 128), BF16),
            v((8, UNITS, 128), BF16),
            v((8, UNITS, 128), BF16),
            v((4, UNITS, 128), BF16),
            v((4, UNITS, 128), BF16),
            v((320, 128), BF16),
            v((320, 128), BF16),
            v((96, 256), F32),
            v((96, 256), F32),
            v((8, 16, 256), BF16),
            v((8, 16, 256), BF16),
            v((8, 16, 256), BF16),
            v((8, 16, 256), BF16),
            v((256, HALF), BF16),
            dma((7,)), dma((5,)), dma((5,)),
            dma((2,)), dma((2,)),
            dma((4, 2, 2)), dma((4, 2)),
            dma((8,)), dma((4,)),
            dma((4, 2, 2)), dma((8, 2)),
            dma((8, 2)), dma((8,)),
            dma((8, 2)), dma((2, 4, 2)),
            dma((4,)), dma((4,)),
            dma((4, 2)), dma((4, 2)),
            dma((4, 2)), dma((4, 2)),
            dma((8,)), dma((8,)),
            dma((8,)), dma((8,)),
            dma((4,)), dma((4,)),
            dma((4,)), dma((4,)),
            dma((8,)), dma((8,)),
            dma((8,)), dma((8,)),
        ],
        compiler_params=pltpu.CompilerParams(
            collective_id=0, has_side_effects=True, vmem_limit_bytes=62 * 1024 * 1024
        ),
    )(hidden, out_grad, weights, table, turn)
    input_grad, weight_grads = pl.pallas_call(
        hand_over,
        out_shape=results,
        in_specs=[hbm, hbm],
        out_specs=(hbm, hbm),
        scratch_shapes=[v((SEQ, 2 * HALF), BF16), v((10, 4, HD), F32), dma((9,)), dma((9,))],
    )(*found)
    return input_grad, jnp.transpose(weight_grads, (1, 0, 2))


def solution(mesh):
    placed = (P(("cuts", "chip"), None), P(("cuts", "chip"), None), P(None, "chip", None))
    return jax.shard_map(
        local,
        mesh=mesh,
        in_specs=placed,
        out_specs=(P(("cuts", "chip"), None), P(None, ("cuts", "chip"), None)),
        check_vma=False,
    )
```
